512 devices in a mesh: ctx: 64 (over x, z, core), head: 8 (over y).
Axes of the slice: x: 4, y: 8, z: 8, core: 2. Of those that a mesh axis runs over, the one named last changes fastest.
Arguments:
- q_lin: bfloat16 [32768, 4096], P('ctx', 'head'), may hold values from -6 to 6
- k_lin: bfloat16 [32768, 4096], P('ctx', 'head'), may hold values from -6 to 6
- v_lin: bfloat16 [32768, 4096], P('ctx', 'head'), may hold values from -30 to 30
- out_gate: bfloat16 [32768, 4096], P('ctx', 'head'), may hold values from -6 to 6
- grad_out: bfloat16 [32768, 4096], P('ctx', 'head'), may hold values from -6 to 6
- log_decay: float32 [32768, 32], P('ctx', 'head'), may hold values from -1 to 0
- norm_gain: float32 [4096], P('head'), may hold values from 0.1 to 1.9
Outputs:
- grad_query: bfloat16 [32768, 4096], P('ctx', 'head')
- grad_key: bfloat16 [32768, 4096], P('ctx', 'head')
- grad_value: bfloat16 [32768, 4096], P('ctx', 'head')
- grad_gate: bfloat16 [32768, 4096], P('ctx', 'head')
The draws below stay inside these ranges and needn't reach their ends.
All inputs are finite; a program needn't handle non-finite values.
Results may differ from the reference program's by a relative error of at most 0.007.
Values sent between devices are 32-bit elements; how exact they have to be, the bound alone decides.
A program may use at most 128 MiB of HBM per device.

```python
import math
import jax
import jax.numpy as jnp
from jax import lax

DH = 128
BLOCK = 512
TOK_DEV = 512
QUERY_HEADS = 32
SEQUENCE_TOKENS = 32768


def draw_log_decay(key, part):
    key = jax.random.fold_in(key, 3)
    order = jax.random.permutation(jax.random.fold_in(key, 1), QUERY_HEADS)
    fast_heads = order < QUERY_HEADS // 2
    slow_rate = jnp.exp(jax.random.uniform(jax.random.fold_in(key, 2), (QUERY_HEADS,), jnp.float32, math.log(0.05), math.log(0.3)))
    spans = jnp.exp(jax.random.uniform(jax.random.fold_in(key, 4), (QUERY_HEADS,), jnp.float32, math.log(20.0), math.log(40.0)))
    decay_rates = jnp.where(fast_heads, 1.0 / spans, slow_rate / SEQUENCE_TOKENS)
    sequence_segment = jnp.exp(jax.random.uniform(jax.random.fold_in(key, 5), (SEQUENCE_TOKENS // TOK_DEV, 1), jnp.float32, -0.69, 0.69))
    sequence_segment = jnp.repeat(sequence_segment, TOK_DEV, axis=0)
    random_offsets = jnp.exp(jax.random.uniform(jax.random.fold_in(key, 6), (SEQUENCE_TOKENS, QUERY_HEADS), jnp.float32, -0.4, 0.4))
    cluster_positions = jax.random.randint(jax.random.fold_in(key, 7), (2,), 0, SEQUENCE_TOKENS)
    cluster_length = jax.random.uniform(jax.random.fold_in(key, 8), (2, QUERY_HEADS), jnp.float32, math.log(0.6), math.log(0.8))
    token_positions = jnp.arange(SEQUENCE_TOKENS)[:, None]
    cluster_starts = jnp.where(token_positions == cluster_positions[0], cluster_length[0][None, :], 0.0) + jnp.where(token_positions == cluster_positions[1], cluster_length[1][None, :], 0.0)
    return -decay_rates[None, :] * sequence_segment * random_offsets + cluster_starts


def draw_v_lin(key, part):
    key = jax.random.fold_in(key, 5)
    column_head = jnp.arange(QUERY_HEADS * DH) // DH
    ramp = 0.6 * 3.0 ** (column_head / max(QUERY_HEADS - 1, 1))
    drawn = jax.random.truncated_normal(jax.random.fold_in(key, 1), -4.0, 4.0, (SEQUENCE_TOKENS, QUERY_HEADS * DH), jnp.float32)
    return (drawn * ramp[None, :]).astype(jnp.bfloat16)


def block_levels(key, shape, pieces, smallest, high):
    gain, own = 1.0, jax.random.fold_in(key, 6)
    for axis_at, shards_of in pieces:
        draws = jnp.exp(jax.random.uniform(jax.random.fold_in(own, axis_at), (shards_of,), jnp.float32, smallest / len(pieces), high / len(pieces)))
        gain = gain * jnp.repeat(draws, shape[axis_at] // shards_of).reshape([-1 if axis == axis_at else 1 for axis in range(len(shape))])
    return gain


def normal_values(stream_key, dims, width, most, split=(), kind=jnp.bfloat16):
    array = width * jax.random.normal(stream_key, dims, jnp.float32)
    if split:
        array = array * block_levels(stream_key, dims, split, -0.22, 0.18)
    return jnp.clip(array, -most, most).astype(kind)


def setup_inputs(seed: int = 0) -> dict:
    splits = jax.random.split(jax.random.key(seed), 8)
    q_lin = normal_values(splits[0], (SEQUENCE_TOKENS, QUERY_HEADS * DH), 1.0, 6.0, ((0, 64), (1, 8)))
    k_lin = normal_values(splits[1], (SEQUENCE_TOKENS, QUERY_HEADS * DH), 1.0, 6.0, ((0, 64), (1, 8)))
    v_lin = draw_v_lin(jax.random.fold_in(splits[7], 71), 0)
    out_gate = normal_values(splits[3], (SEQUENCE_TOKENS, QUERY_HEADS * DH), 1.0, 6.0, ((0, 64), (1, 8)))
    grad_out = normal_values(splits[4], (SEQUENCE_TOKENS, QUERY_HEADS * DH), 1.0, 6.0, ((0, 64), (1, 8)))
    log_decay = draw_log_decay(jax.random.fold_in(splits[7], 71), 0)
    norm_gain = jnp.clip(1.0 + 0.18 * jax.random.normal(splits[6], (QUERY_HEADS * DH,), jnp.float32), 0.1, 1.9)
    return {"q_lin": q_lin, "k_lin": k_lin, "v_lin": v_lin, "out_gate": out_gate, "grad_out": grad_out, "log_decay": log_decay, "norm_gain": norm_gain}


def rounded(values):
    return lax.optimization_barrier(values.astype(jnp.bfloat16)).astype(jnp.float32)

def decay_block(cumul, lower_tri):
    trans = cumul.T
    diff = trans[:, :, None] - trans[:, None, :]
    return jnp.where(lower_tri[None], jnp.exp(jnp.where(lower_tri[None], diff, 0.0)), 0.0)

def chain_step(carried, inputs):
    decays, local_terms = inputs
    return (decays[:, None, None] * carried + local_terms, carried)

def reference(q_lin, k_lin, v_lin, out_gate, grad_out, log_decay, norm_gain):
    num_blocks = SEQUENCE_TOKENS // BLOCK
    block_shape = (num_blocks, BLOCK, QUERY_HEADS, DH)
    queries = q_lin.astype(jnp.float32).reshape(block_shape)
    keyed = k_lin.astype(jnp.float32).reshape(block_shape)
    valued = v_lin.astype(jnp.float32).reshape(block_shape)
    cumul = jnp.cumsum(log_decay.reshape(num_blocks, BLOCK, QUERY_HEADS), axis=1)
    totals = cumul[:, -1, :]
    tail_decay = jnp.exp(totals[:, None, :] - cumul)
    head_decay = jnp.exp(cumul)
    lower_tri = jnp.arange(BLOCK)[:, None] >= jnp.arange(BLOCK)[None, :]
    zero_state = jnp.zeros((QUERY_HEADS, DH, DH), jnp.float32)
    weighted_key = rounded(keyed * tail_decay[..., None])
    block_state = jnp.einsum('nbhk,nbhv->nhkv', weighted_key, valued)
    _, entering = lax.scan(chain_step, zero_state, (jnp.exp(totals), block_state))
    entering_b = rounded(entering)

    def forward_block(inputs):
        query_block, key_block, value_block, cumulative_block_decay, forward_block_state = inputs
        decays = decay_block(cumulative_block_decay, lower_tri)
        weights = rounded(jnp.einsum('thd,shd->hts', query_block, key_block) * decays)
        intra = jnp.einsum('aob,bae->oae', weights, value_block)
        between_blocks_term = jnp.einsum('yrn,rnm->yrm', query_block, forward_block_state) * jnp.exp(cumulative_block_decay)[..., None]
        return intra + between_blocks_term
    attended = lax.map(forward_block, (queries, keyed, valued, cumul, entering_b))
    attended = attended.reshape(SEQUENCE_TOKENS, QUERY_HEADS * DH)
    features = QUERY_HEADS * DH
    rms_inv = lax.rsqrt(lax.optimization_barrier(jnp.sum(attended * attended, axis=1, keepdims=True)) / features + 1e-05)
    gate_sig = jax.nn.sigmoid(out_gate.astype(jnp.float32))
    grad_o = grad_out.astype(jnp.float32)
    grad_gate = (grad_o * attended * rms_inv * norm_gain[None, :] * gate_sig * (1.0 - gate_sig)).astype(jnp.bfloat16)
    grad_normed = grad_o * gate_sig * norm_gain[None, :]
    inner_sum = lax.optimization_barrier(jnp.sum(grad_normed * attended, axis=1, keepdims=True))
    grad_attn = rounded(rms_inv * grad_normed - attended * rms_inv ** 3 * inner_sum / features)
    grad_blk = grad_attn.reshape(block_shape)
    weighted_query = rounded(queries * head_decay[..., None])
    block_reverse = jnp.einsum('nbhk,nbhv->nhkv', weighted_query, grad_blk)
    _, leaving = lax.scan(chain_step, zero_state, (jnp.exp(totals), block_reverse), reverse=True)
    leaving_b = rounded(leaving)

    def backward_block(inputs):
        query_block, key_block, value_block, gate_block, cumulative_block_decay, block_tail_decay, forward_block_state, reverse_block_state = inputs
        decays = decay_block(cumulative_block_decay, lower_tri)
        forward_decay_weights = rounded(jnp.einsum('thd,shd->hts', query_block, key_block) * decays)
        reverse_decay_weights = rounded(jnp.einsum('thd,shd->hts', gate_block, value_block) * decays)
        query_gradient = jnp.einsum('aob,bae->oae', reverse_decay_weights, key_block) + jnp.exp(cumulative_block_decay)[..., None] * jnp.einsum('spm,pdm->spd', gate_block, forward_block_state)
        key_gradient = jnp.einsum('zpv,pzx->vzx', reverse_decay_weights, query_block) + block_tail_decay[..., None] * jnp.einsum('xqb,qcb->xqc', value_block, reverse_block_state)
        value_gradient = jnp.einsum('zpv,pzx->vzx', forward_decay_weights, gate_block) + block_tail_decay[..., None] * jnp.einsum('zne,neb->znb', key_block, reverse_block_state)
        return (query_gradient.astype(jnp.bfloat16), key_gradient.astype(jnp.bfloat16), value_gradient.astype(jnp.bfloat16))
    query_gradient, key_gradient, value_gradient = lax.map(backward_block, (queries, keyed, valued, grad_blk, cumul, tail_decay, entering_b, leaving_b))
    grad_query = query_gradient.reshape(SEQUENCE_TOKENS, QUERY_HEADS * DH)
    grad_key = key_gradient.reshape(SEQUENCE_TOKENS, QUERY_HEADS * DH)
    grad_value = value_gradient.reshape(SEQUENCE_TOKENS, QUERY_HEADS * DH)
    return (grad_query, grad_key, grad_value, grad_gate)
```

```python
import functools

import jax
import jax.numpy as jnp
from jax import lax
from jax.experimental import pallas as pl
from jax.experimental.pallas import tpu as pltpu
from jax.sharding import PartitionSpec as P

BLOCK = 512
DH = 128
HEADS = 4
HALF = HEADS // 2 * DH
TILE = 256
NX = 4
NZ = 8
F32 = jnp.float32
BF16 = jnp.bfloat16
MESH = pl.DeviceIdType.MESH


def nn(a, b):
    return jnp.dot(a, b, preferred_element_type=F32)


def nt(a, b):
    return lax.dot_general(a, b, (((1,), (1,)), ((), ())), preferred_element_type=F32)


def lane_cumsum(x):
    place = lax.broadcasted_iota(jnp.int32, x.shape, 1)
    step = 1
    while step < x.shape[1]:
        x = x + jnp.where(place >= step, pltpu.roll(x, step, 1), 0.0)
        step *= 2
    return x


def columns(row):
    return jnp.broadcast_to(row, (DH, row.shape[1])).T


def kernel(
    nx, nz, nh,
    q_hbm, k_hbm, v_hbm, gate_hbm, gout_hbm, ld_hbm, gain_hbm,
    dq_hbm, dk_hbm, dv_hbm, dg_hbm,
    q, k, v, gate, gout, ld, gain,
    dq, dk, dv, dg,
    a_row, ea_row, tail_row, ea_col, tail_col,
    qt, wqt, wq, wk, wv, mask, fw, att, gn, gg, gb, dki, dvi,
    f_own, f_par, f_chip, f_zin, f_xout, f_xin, f_back, f_ent, f_pair, f_state,
    r_own, r_par, r_chip, r_zin, r_xout, r_xin, r_back, r_ent, r_pair, r_state,
    y_out, y_in,
    local_sem, send_sem, recv_sem,
):
    me, head = lax.axis_index("ctx"), lax.axis_index("head")
    core, z, x = me % 2, (me // 2) % nz, me // (2 * nz)
    rows = HALF // nz

    def at(xx, zz, cc):
        return ((xx * nz + zz) * 2 + cc, head)

    partner = at(x, z, 1 - core)
    z_peers = [at(x, (z + d) % nz, core) for d in range(1, nz)]
    x_peers = [at((x + d) % nx, z, core) for d in range(1, nx)]
    y_peers = [(me, (head + d) % nh) for d in range(1, nh)]

    loads = {}
    for i, (name, src, dst) in enumerate((
        ("ld", ld_hbm, ld), ("k", k_hbm, k), ("v", v_hbm, v), ("q", q_hbm, q),
        ("gate", gate_hbm, gate), ("gout", gout_hbm, gout), ("gain", gain_hbm, gain),
    )):
        loads[name] = pltpu.make_async_copy(src, dst, local_sem.at[i])
        loads[name].start()
    barrier = pltpu.get_barrier_semaphore()
    peers = [partner] + z_peers + x_peers + y_peers
    for peer in peers:
        pl.semaphore_signal(barrier, inc=1, device_id=peer, device_id_type=MESH)

    started = []
    count = [0]

    def send(src, dst, device):
        copy = pltpu.make_async_remote_copy(
            src_ref=src, dst_ref=dst, send_sem=send_sem.at[count[0]],
            recv_sem=recv_sem.at[count[0]], device_id=device, device_id_type=MESH,
        )
        count[0] += 1
        copy.start()
        started.append(copy)
        return copy

    def arrived(copies):
        for copy in copies:
            copy.wait_recv()

    def lanes(h):
        return slice(h * DH, (h + 1) * DH)

    def stage_pair(own, par):
        return [send(own.at[1 - core], par, partner)]

    def first(reverse):
        return (core == 1) if reverse else (core == 0)

    def totals():
        tile_own = f_own[core, HALF:, :]
        tile_par = f_par[HALF:, :]
        return tile_own, tile_par

    def stage_chip(own, par, chip, zin, reverse):
        tile_own, tile_par = totals()
        one = jnp.ones_like(tile_own)
        w_own = jnp.where(first(reverse), jnp.exp(tile_par), one)
        w_par = jnp.where(first(reverse), one, jnp.exp(tile_own))
        both = jnp.exp(tile_own + tile_par)
        for zz in range(nz):
            at_row = zz * rows
            t = 4 * (at_row // DH)
            chip[zz, :rows, :] = (
                w_own[t : t + 1] * own[core, at_row : at_row + rows, :]
                + w_par[t : t + 1] * par[at_row : at_row + rows, :]
            )
            if not reverse:
                chip[zz, rows:, :] = jnp.broadcast_to(both[t : t + 1], (8, DH))
        zin[z] = chip[z]
        return [
            send(chip.at[(z + d) % nz], zin.at[z], z_peers[d - 1]) for d in range(1, nz)
        ]

    def order(n, reverse):
        return list(reversed(range(n))) if reverse else list(range(n))

    def stage_row(zin, xout, xin, state, reverse):
        total = jnp.zeros((rows, DH), F32)
        decay = jnp.ones((1, DH), F32)
        for zz in order(nz, reverse):
            state[zz, :rows, :] = total
            state[zz, rows:, :] = jnp.broadcast_to(decay, (8, DH))
            step = f_zin[zz, rows : rows + 1, :]
            total = step * total + zin[zz, :rows, :]
            decay = step * decay
        xout[:rows, :] = total
        xin[x, :rows, :] = total
        if not reverse:
            xout[rows:, :] = jnp.broadcast_to(decay, (8, DH))
            xin[x, rows:, :] = jnp.broadcast_to(decay, (8, DH))
        return [send(xout, xin.at[x], peer) for peer in x_peers]

    def stage_carry(xin, chip, back, state, reverse):
        carry = jnp.zeros((rows, DH), F32)
        for xx in order(nx, reverse):
            ahead = (xx > x) if reverse else (xx < x)
            step = f_xin[xx, rows : rows + 1, :]
            carry = jnp.where(ahead, step * carry + xin[xx, :rows, :], carry)
        for zz in range(nz):
            state[zz, :rows, :] = state[zz, :rows, :] + state[zz, rows : rows + 1, :] * carry
        back[z] = state[z, :rows, :]
        return [
            send(state.at[(z + d) % nz, pl.ds(0, rows)], back.at[z], z_peers[d - 1])
            for d in range(1, nz)
        ]

    def stage_split(own, par, back, ent, pair, reverse):
        tile_own, tile_par = totals()
        one, zero = jnp.ones_like(tile_own), jnp.zeros_like(tile_own)
        lead = first(reverse)
        w_own = jnp.where(lead, one, jnp.exp(tile_par))
        s_own = jnp.where(lead, zero, one)
        w_par = jnp.where(lead, jnp.exp(tile_own), one)
        s_par = jnp.where(lead, one, zero)
        for zz in range(nz):
            at_row = zz * rows
            t = 4 * (at_row // DH)
            here = slice(at_row, at_row + rows)
            entering = back[zz]
            pair[here, :] = (
                w_par[t : t + 1] * entering + s_par[t : t + 1] * own[core, here, :]
            )
        copies = [send(pair, ent.at[core], partner)]
        for zz in range(nz):
            at_row = zz * rows
            t = 4 * (at_row // DH)
            here = slice(at_row, at_row + rows)
            ent[core, here, :] = (
                w_own[t : t + 1] * back[zz] + s_own[t : t + 1] * par[here, :]
            )
        return copies

    loads["ld"].wait()
    cumul = lane_cumsum(jnp.concatenate([ld[...], ld[...]], axis=0))
    total = cumul[:, BLOCK - 1 :]
    a_row[...] = cumul
    ea_row[...] = jnp.exp(cumul)
    tail_row[...] = jnp.exp(total - cumul)
    for h in range(HEADS):
        f_own[h // 2, HALF + 4 * (h % 2) : HALF + 4 * (h % 2) + 4, :] = jnp.broadcast_to(
            total[h : h + 1], (4, DH)
        )

    loads["k"].wait()
    loads["v"].wait()
    for h in range(HEADS):
        weighted = (k[:, lanes(h)].T.astype(F32) * tail_row[h : h + 1, :]).astype(BF16)
        f_own[h // 2, (h % 2) * DH : (h % 2 + 1) * DH, :] = nn(weighted, v[:, lanes(h)])
    pl.semaphore_wait(barrier, len(peers))
    copies = stage_pair(f_own, f_par)

    def prepare(h):
        ea = columns(ea_row[h : h + 1, :])
        tail = columns(tail_row[h : h + 1, :])
        ea_col[h] = ea
        q_here = q[:, lanes(h)]
        wq[h] = (q_here.astype(F32) * ea).astype(BF16)
        wk[h] = (k[:, lanes(h)].astype(F32) * tail).astype(BF16)
        wv[h] = (v[:, lanes(h)].astype(F32) * tail).astype(BF16)
        qt[h] = q_here.T
        wqt[h] = (qt[h].astype(F32) * ea_row[h : h + 1, :]).astype(BF16)

    def intra(h):
        a_here = a_row[h : h + 1, :]
        a_col = columns(a_here)
        for t in range(0, BLOCK, TILE):
            seen = t + TILE
            here = slice(t, seen)
            scores = nt(q[here, lanes(h)], k[:seen, lanes(h)])
            col = jnp.concatenate([a_col[here]] * (seen // DH), axis=1)
            diff = col - a_here[:, :seen]
            keep = lax.broadcasted_iota(jnp.int32, diff.shape, 0) + t >= (
                lax.broadcasted_iota(jnp.int32, diff.shape, 1)
            )
            decay = jnp.where(keep, jnp.exp(jnp.where(keep, diff, 0.0)), 0.0)
            mask[h, here, :seen] = decay
            weights = (scores * decay).astype(BF16)
            fw[h, here, :seen] = weights
            att[here, lanes(h)] = nn(weights, v[:seen, lanes(h)])

    def gates(h):
        sig = jax.nn.sigmoid(gate[:, lanes(h)].astype(F32))
        normed = gout[:, lanes(h)].astype(F32) * sig * gain[:, lanes(h)]
        gn[:, lanes(h)] = normed
        gg[:, lanes(h)] = normed * (1.0 - sig)

    loads["q"].wait()
    prepare(0)
    intra(0)
    arrived(copies)
    copies = stage_chip(f_own, f_par, f_chip, f_zin, False)
    prepare(1)
    intra(1)
    prepare(2)
    intra(2)
    arrived(copies)
    copies = stage_row(f_zin, f_xout, f_xin, f_state, False)
    prepare(3)
    intra(3)
    arrived(copies)
    copies = stage_carry(f_xin, f_chip, f_back, f_state, False)
    for name in ("gate", "gout", "gain"):
        loads[name].wait()
    for h in range(HEADS):
        gates(h)
    arrived(copies)
    copies = stage_split(f_own, f_par, f_back, f_ent, f_pair, False)
    arrived(copies)

    def state_b(ent, h):
        return ent[h // 2, (h % 2) * DH : (h % 2 + 1) * DH, :].astype(BF16)

    squares = jnp.zeros((BLOCK, DH), F32)
    inner = jnp.zeros((BLOCK, DH), F32)
    for h in range(HEADS):
        full = att[:, lanes(h)] + nn(wq[h], state_b(f_ent, h))
        att[:, lanes(h)] = full
        squares = squares + full * full
        inner = inner + full * gn[:, lanes(h)]

    ones = jnp.ones((8, DH), BF16)

    def row_sums(value):
        high = value.astype(BF16)
        low = (value - high.astype(F32)).astype(BF16)
        return nt(ones, high) + nt(ones, low)

    sums = [row_sums(squares), row_sums(inner)]
    parts = BLOCK // DH
    y_out[...] = jnp.concatenate(
        [s[0:1, i * DH : (i + 1) * DH] for s in sums for i in range(parts)], axis=0
    )
    y_in[head] = y_out[...]
    copies = [send(y_out, y_in.at[head], peer) for peer in y_peers]
    arrived(copies)
    summed = y_in[0]
    for i in range(1, nh):
        summed = summed + y_in[i]
    features = HEADS * DH * nh
    rms = lax.rsqrt(summed[:parts] / features + 1e-05)
    coef = rms * rms * rms * summed[parts:] / features
    rms_col = jnp.concatenate([columns(rms[i : i + 1]) for i in range(parts)], axis=0)
    coef_col = jnp.concatenate([columns(coef[i : i + 1]) for i in range(parts)], axis=0)
    for h in range(HEADS):
        grad = (rms_col * gn[:, lanes(h)] - att[:, lanes(h)] * coef_col).astype(BF16)
        gb[:, lanes(h)] = grad
        r_own[h // 2, (h % 2) * DH : (h % 2 + 1) * DH, :] = nn(wqt[h], grad)
    copies = stage_pair(r_own, r_par)

    stores = []

    def store(src, dst):
        copy = pltpu.make_async_copy(src, dst, local_sem.at[7 + len(stores)])
        copy.start()
        stores.append(copy)

    def back(h):
        grad = gb[:, lanes(h)]
        entering = state_b(f_ent, h)
        upper = []
        for t in range(0, BLOCK, TILE):
            seen = t + TILE
            here = slice(t, seen)
            weights = (nt(grad[here], v[:seen, lanes(h)]) * mask[h, here, :seen]).astype(BF16)
            upper.append(weights)
            dq[here, lanes(h)] = (
                nn(weights, k[:seen, lanes(h)]) + ea_col[h, here, :] * nt(grad[here], entering)
            ).astype(BF16)
        gt = grad.T
        for s in range(0, BLOCK, TILE):
            here = slice(s, s + TILE)
            key = value = None
            for t in range(s, BLOCK, TILE):
                there = slice(t, t + TILE)
                one_key = nn(qt[h, :, there], upper[t // TILE][:, here])
                one_value = nn(gt[:, there], fw[h, there, here])
                key = one_key if key is None else key + one_key
                value = one_value if value is None else value + one_value
            dki[here, lanes(h)] = key.T
            dvi[here, lanes(h)] = value.T

    back(0)
    arrived(copies)
    copies = stage_chip(r_own, r_par, r_chip, r_zin, True)
    back(1)
    back(2)
    arrived(copies)
    copies = stage_row(r_zin, r_xout, r_xin, r_state, True)
    back(3)
    arrived(copies)
    copies = stage_carry(r_xin, r_chip, r_back, r_state, True)
    store(dq, dq_hbm)
    for h in range(HEADS):
        dg[:, lanes(h)] = (gg[:, lanes(h)] * att[:, lanes(h)] * rms_col).astype(BF16)
    store(dg, dg_hbm)
    arrived(copies)
    copies = stage_split(r_own, r_par, r_back, r_ent, r_pair, True)
    arrived(copies)
    for h in range(HEADS):
        leaving = state_b(r_ent, h)
        dk[:, lanes(h)] = (dki[:, lanes(h)] + nt(wv[h], leaving)).astype(BF16)
        dv[:, lanes(h)] = (dvi[:, lanes(h)] + nn(wk[h], leaving)).astype(BF16)
    store(dk, dk_hbm)
    store(dv, dv_hbm)
    for copy in started:
        copy.wait_send()
    for copy in stores:
        copy.wait()


def build(nx, nz, nh):
    rows = HALF // nz
    wide = (BLOCK, HEADS * DH)
    per_head = (HEADS, BLOCK, DH)

    def vmem(shape, dtype=F32):
        return pltpu.VMEM(shape, dtype)

    def scan_scratch(extra):
        return [
            vmem((2, HALF + extra, DH)),
            vmem((HALF + extra, DH)),
            vmem((nz, rows + extra, DH)),
            vmem((nz, rows + extra, DH)),
            vmem((rows + extra, DH)),
            vmem((nx, rows + extra, DH)),
            vmem((nz, rows, DH)),
            vmem((2, HALF, DH)),
            vmem((HALF, DH)),
            vmem((nz, rows + 8, DH)),
        ]

    n_copies = 2 * (2 + 2 * (nz - 1) + nx - 1) + nh - 1
    scratch = (
        [vmem(wide, BF16)] * 5
        + [vmem((HEADS, BLOCK)), vmem((1, HEADS * DH))]
        + [vmem(wide, BF16)] * 4
        + [vmem((8, BLOCK))] * 3
        + [vmem(per_head)] * 2
        + [vmem((HEADS, DH, BLOCK), BF16)] * 2
        + [vmem(per_head, BF16)] * 3
        + [vmem((HEADS, BLOCK, BLOCK)), vmem((HEADS, BLOCK, BLOCK), BF16)]
        + [vmem(wide)] * 3
        + [vmem(wide, BF16)]
        + [vmem(wide)] * 2
        + scan_scratch(8)
        + scan_scratch(0)
        + [vmem((8, DH)), vmem((nh, 8, DH))]
        + [
            pltpu.SemaphoreType.DMA((11,)),
            pltpu.SemaphoreType.DMA((n_copies,)),
            pltpu.SemaphoreType.DMA((n_copies,)),
        ]
    )

    def local(q, k, v, gate, gout, log_decay, gain):
        any_space = pl.BlockSpec(memory_space=pl.ANY)
        return tuple(
            pl.pallas_call(
                functools.partial(kernel, nx, nz, nh),
                out_shape=[jax.ShapeDtypeStruct(wide, BF16)] * 4,
                in_specs=[any_space] * 7,
                out_specs=[any_space] * 4,
                scratch_shapes=scratch,
                compiler_params=pltpu.CompilerParams(
                    collective_id=0, has_side_effects=True, vmem_limit_bytes=56 * 2**20
                ),
            )(q, k, v, gate, gout, log_decay.T, gain.reshape(1, HEADS * DH))
        )

    return local


def solution(mesh):
    nx, nz = NX, NZ
    if mesh.shape["ctx"] != 2 * nx * nz:
        nx = nz = 2
    part = P("ctx", "head")
    return jax.shard_map(
        build(nx, nz, mesh.shape["head"]),
        mesh=mesh,
        in_specs=(part,) * 6 + (P("head"),),
        out_specs=(part,) * 4,
        check_vma=False,
    )
```

```python
import functools

import jax
import jax.numpy as jnp
from jax import lax
from jax.experimental import pallas as pl
from jax.experimental.pallas import tpu as pltpu
from jax.sharding import PartitionSpec as P

BLOCK = 512
DH = 128
HEADS = 4
HALF = HEADS // 2
TILE = 256
NX = 4
NZ = 8
F32 = jnp.float32
BF16 = jnp.bfloat16
MESH = pl.DeviceIdType.MESH


def nn(a, b):
    return jnp.dot(a, b, preferred_element_type=F32)


def nt(a, b):
    return lax.dot_general(a, b, (((1,), (1,)), ((), ())), preferred_element_type=F32)


def lane_cumsum(x):
    place = lax.broadcasted_iota(jnp.int32, x.shape, 1)
    step = 1
    while step < x.shape[1]:
        x = x + jnp.where(place >= step, pltpu.roll(x, step, 1), 0.0)
        step *= 2
    return x


def turned(rows):
    pad = jnp.zeros((DH - rows.shape[0], rows.shape[1]), F32)
    return jnp.concatenate([rows, pad], axis=0).T


def kept(shape, dtype):
    return pltpu.VMEM(shape, dtype)


def placed(values, space):
    return [pltpu.with_memory_space_constraint(value, space) for value in values]


def lanes(h):
    return slice(h * DH, (h + 1) * DH)


def kernel(
    nx, nz, nh,
    q_hbm, k_hbm, v_hbm, gate_hbm, gout_hbm, ld_hbm, gain_hbm,
    dq, dg, dki, dvi, wk, wv, r_ent,
    q, k, v, gate, gout, ld, gain,
    row_form, col_form, ea_col,
    qt, wqt, wq, mask, fw, att, gn, gg, gb,
    g_own, g_par, g_all, decay,
    f_own, f_par, f_chip, f_zin, f_back, f_ent, f_pair, f_pre,
    r_own, r_par, r_chip, r_zin, r_back, r_pair, r_pre,
    y_out, y_in,
    local_sem, send_sem, recv_sem,
):
    me, head = lax.axis_index("ctx"), lax.axis_index("head")
    core, chip_at = me % 2, me // 2
    z, x = chip_at % nz, chip_at // nz
    chips = nx * nz
    rows = HALF * DH // chips
    per_head = chips // HALF

    def at(xx, zz, cc):
        return ((xx * nz + zz) * 2 + cc, head)

    partner = at(x, z, 1 - core)
    far_first = sorted(range(nz), key=lambda d: -min(d, nz - d))
    steps = [(dx, dz) for dz in far_first for dx in range(nx) if (dx, dz) != (0, 0)]
    others = [((x + dx) % nx, (z + dz) % nz) for dx, dz in steps]
    z_peers = [at(x, (z + d) % nz, core) for d in range(1, nz)]
    x_peers = [at((x + d) % nx, z, core) for d in range(1, nx)]
    chip_peers = [at(xx, zz, core) for xx, zz in others]
    y_peers = [(me, (head + d) % nh) for d in range(1, nh)]

    loads = {}
    for i, (name, src, dst) in enumerate((
        ("ld", ld_hbm, ld), ("k", k_hbm, k), ("v", v_hbm, v), ("q", q_hbm, q),
        ("gate", gate_hbm, gate), ("gout", gout_hbm, gout), ("gain", gain_hbm, gain),
    )):
        loads[name] = pltpu.make_async_copy(src, dst, local_sem.at[i])
        loads[name].start()
    barrier = pltpu.get_barrier_semaphore()
    peers = [partner] + chip_peers + y_peers
    for peer in peers:
        pl.semaphore_signal(barrier, inc=1, device_id=peer, device_id_type=MESH)

    sent = []
    stage = [0]

    def send(copies, span):
        mine, stage[0] = stage[0], stage[0] + 1
        for src, dst, device in copies:
            pltpu.make_async_remote_copy(
                src_ref=src, dst_ref=dst, send_sem=send_sem.at[mine],
                recv_sem=recv_sem.at[mine], device_id=device, device_id_type=MESH,
            ).start()
        sent.append((mine, span))
        return mine, span

    def arrived(handle):
        mine, span = handle
        pltpu.make_async_copy(span, span, recv_sem.at[mine]).wait()

    def first(reverse):
        return (core == 1) if reverse else (core == 0)

    def decay_row(ref, i):
        return jnp.exp(ref[pl.ds(HALF * core + i, 1), :])

    def part(i):
        return slice(i * per_head, (i + 1) * per_head)

    def stage_pair(own, par):
        return send([(own.at[1 - core], par, partner)], par)

    def stage_chip(own, par, chip, zin, reverse):
        one = jnp.ones((1, DH), F32)
        for i in range(HALF):
            w_own = jnp.where(first(reverse), decay_row(g_par, i), one)
            w_par = jnp.where(first(reverse), one, decay_row(g_own, i))
            chip[part(i)] = w_own * own[core, part(i)] + w_par * par[part(i)]
        handle = send(
            [
                (chip.at[xx * nz + zz], zin.at[chip_at], device)
                for (xx, zz), device in zip(others, chip_peers)
            ],
            zin.at[pl.ds(0, chips - 1)],
        )
        zin[chip_at] = chip[chip_at]
        return handle

    def stage_fold(zin, pre, back, reverse):
        total = jnp.zeros((rows, DH), F32)
        for j in reversed(range(chips)) if reverse else range(chips):
            pre[j] = total
            total = decay[j, 0:1, :] * total + zin[j]
        handle = send(
            [
                (pre.at[xx * nz + zz], back.at[chip_at], device)
                for (xx, zz), device in zip(others, chip_peers)
            ],
            back.at[pl.ds(0, chips - 1)],
        )
        back[chip_at] = pre[chip_at]
        return handle

    def stage_split(own, par, back, ent, pair, reverse):
        one, zero = jnp.ones((1, DH), F32), jnp.zeros((1, DH), F32)
        lead = first(reverse)
        for i in range(HALF):
            w_par = jnp.where(lead, decay_row(g_own, i), one)
            s_par = jnp.where(lead, one, zero)
            pair[part(i)] = w_par * back[part(i)] + s_par * own[core, part(i)]
        handle = send([(pair, ent.at[core], partner)], pair)
        for i in range(HALF):
            w_own = jnp.where(lead, one, decay_row(g_par, i))
            s_own = jnp.where(lead, zero, one)
            ent[core, part(i)] = w_own * back[part(i)] + s_own * par[part(i)]
        return handle

    def state_b(ent, h):
        return ent[h // HALF, part(h % HALF)].reshape(DH, DH).astype(BF16)

    loads["ld"].wait()
    cumul = lane_cumsum(jnp.concatenate([ld[...], ld[...]], axis=0))
    total = cumul[:, BLOCK - 1 :]
    g_own[...] = jnp.broadcast_to(total, (8, DH))
    ea, tail = jnp.exp(cumul), jnp.exp(total - cumul)
    row_form[0], row_form[1], row_form[2] = cumul, ea, tail
    pl.semaphore_wait(barrier, len(peers))
    g_copies = send([(g_own, g_par, partner)], g_par)

    loads["k"].wait()
    loads["v"].wait()
    for h in range(HEADS):
        weighted = (k[:, lanes(h)].T.astype(F32) * tail[h : h + 1, :]).astype(BF16)
        f_own[h // HALF, part(h % HALF)] = nn(weighted, v[:, lanes(h)]).reshape(
            per_head, rows, DH
        )
    copies = stage_pair(f_own, f_par)
    arrived(g_copies)
    g_all[chip_at] = g_own[...] + g_par[...]
    g_copies = send(
        [(g_all.at[chip_at], g_all.at[chip_at], peer) for peer in z_peers],
        g_all.at[pl.ds(0, nz - 1)],
    )

    col_form[...] = turned(jnp.concatenate([cumul, ea, tail], axis=0))

    def column(kind, h):
        j = 8 * kind + h
        return jnp.broadcast_to(col_form[:, j : j + 1], (BLOCK, DH))

    def prepare(h):
        ea_here = column(1, h)
        tail_here = column(2, h)
        ea_col[h] = ea_here
        q_here = q[:, lanes(h)]
        wq[h] = (q_here.astype(F32) * ea_here).astype(BF16)
        wk[:, lanes(h)] = (k[:, lanes(h)].astype(F32) * tail_here).astype(BF16)
        wv[:, lanes(h)] = (v[:, lanes(h)].astype(F32) * tail_here).astype(BF16)
        turned_q = q_here.T
        qt[h] = turned_q
        wqt[h] = (turned_q.astype(F32) * row_form[1, h : h + 1, :]).astype(BF16)

    def intra(h):
        a_here = row_form[0, h : h + 1, :]
        a_col = column(0, h)
        for t in range(0, BLOCK, TILE):
            seen = t + TILE
            here = slice(t, seen)
            scores = nt(q[here, lanes(h)], k[:seen, lanes(h)])
            col = jnp.concatenate([a_col[here]] * (seen // DH), axis=1)
            diff = col - a_here[:, :seen]
            keep = lax.broadcasted_iota(jnp.int32, diff.shape, 0) + t >= (
                lax.broadcasted_iota(jnp.int32, diff.shape, 1)
            )
            weight = jnp.where(keep, jnp.exp(jnp.where(keep, diff, 0.0)), 0.0)
            mask[h, here, :seen] = weight
            weights = (scores * weight).astype(BF16)
            fw[h, here, :seen] = weights
            att[here, lanes(h)] = nn(weights, v[:seen, lanes(h)])

    def gates(h):
        sig = jax.nn.sigmoid(gate[:, lanes(h)].astype(F32))
        normed = gout[:, lanes(h)].astype(F32) * sig * gain[:, lanes(h)]
        gn[:, lanes(h)] = normed
        gg[:, lanes(h)] = normed * (1.0 - sig)

    loads["q"].wait()
    prepare(0)
    arrived(g_copies)
    row_at = pl.ds(x * nz, nz)
    g_copies = send(
        [(g_all.at[row_at], g_all.at[row_at], peer) for peer in x_peers],
        g_all.at[pl.ds(0, nz * (nx - 1))],
    )
    arrived(copies)
    copies = stage_chip(f_own, f_par, f_chip, f_zin, False)
    intra(0)
    prepare(1)
    intra(1)
    prepare(2)
    intra(2)
    arrived(g_copies)
    mine = HALF * core + chip_at * rows // DH
    for j in range(chips):
        decay[j] = jnp.broadcast_to(jnp.exp(g_all[j, pl.ds(mine, 1), :]), (8, DH))
    arrived(copies)
    copies = stage_fold(f_zin, f_pre, f_back, False)
    prepare(3)
    intra(3)
    for name in ("gate", "gout", "gain"):
        loads[name].wait()
    for h in range(HEADS):
        gates(h)
    arrived(copies)
    copies = stage_split(f_own, f_par, f_back, f_ent, f_pair, False)
    arrived(copies)

    squares = jnp.zeros((BLOCK, DH), F32)
    inner = jnp.zeros((BLOCK, DH), F32)
    for h in range(HEADS):
        full = att[:, lanes(h)] + nn(wq[h], state_b(f_ent, h))
        att[:, lanes(h)] = full
        squares = squares + full * full
        inner = inner + full * gn[:, lanes(h)]

    ones = jnp.ones((8, DH), BF16)

    def row_sums(value):
        high = value.astype(BF16)
        low = (value - high.astype(F32)).astype(BF16)
        return nt(ones, high) + nt(ones, low)

    sums = [row_sums(squares), row_sums(inner)]
    parts = BLOCK // DH
    y_out[...] = jnp.concatenate(
        [s[0:1, i * DH : (i + 1) * DH] for s in sums for i in range(parts)], axis=0
    )
    copies = send(
        [(y_out, y_in.at[head], peer) for peer in y_peers], y_in.at[pl.ds(0, nh - 1)]
    )
    y_in[head] = y_out[...]
    arrived(copies)
    summed = y_in[0]
    for i in range(1, nh):
        summed = summed + y_in[i]
    features = HEADS * DH * nh
    rms = lax.rsqrt(summed[:parts] / features + 1e-05)
    coef = rms * rms * rms * summed[parts:] / features
    scales = turned(jnp.concatenate([rms, coef], axis=0))

    def scale_column(first_lane):
        return jnp.concatenate(
            [
                jnp.broadcast_to(scales[:, i : i + 1], (DH, DH))
                for i in range(first_lane, first_lane + parts)
            ],
            axis=0,
        )

    rms_col, coef_col = scale_column(0), scale_column(parts)
    for h in range(HEADS):
        grad = (rms_col * gn[:, lanes(h)] - att[:, lanes(h)] * coef_col).astype(BF16)
        gb[:, lanes(h)] = grad
        r_own[h // HALF, part(h % HALF)] = nn(wqt[h], grad).reshape(per_head, rows, DH)
    copies = stage_pair(r_own, r_par)

    def back(h):
        grad = gb[:, lanes(h)]
        entering = state_b(f_ent, h)
        upper = []
        for t in range(0, BLOCK, TILE):
            seen = t + TILE
            here = slice(t, seen)
            weights = (nt(grad[here], v[:seen, lanes(h)]) * mask[h, here, :seen]).astype(BF16)
            upper.append(weights)
            dq[here, lanes(h)] = (
                nn(weights, k[:seen, lanes(h)]) + ea_col[h, here, :] * nt(grad[here], entering)
            ).astype(BF16)
        gt = grad.T
        for s in range(0, BLOCK, TILE):
            here = slice(s, s + TILE)
            key = value = None
            for t in range(s, BLOCK, TILE):
                there = slice(t, t + TILE)
                one_key = nn(qt[h, :, there], upper[t // TILE][:, here])
                one_value = nn(gt[:, there], fw[h, there, here])
                key = one_key if key is None else key + one_key
                value = one_value if value is None else value + one_value
            dki[here, lanes(h)] = key.T
            dvi[here, lanes(h)] = value.T

    for h in range(HEADS):
        dg[:, lanes(h)] = (gg[:, lanes(h)] * att[:, lanes(h)] * rms_col).astype(BF16)
    arrived(copies)
    copies = stage_chip(r_own, r_par, r_chip, r_zin, True)
    back(0)
    back(1)
    arrived(copies)
    copies = stage_fold(r_zin, r_pre, r_back, True)
    back(2)
    back(3)
    arrived(copies)
    copies = stage_split(r_own, r_par, r_back, r_ent, r_pair, True)
    arrived(copies)
    for mine, span in sent:
        pltpu.make_async_copy(span, span, send_sem.at[mine]).wait()


def finish(
    dq_in, dg_in, dki, dvi, wk, wv, ent, dq_hbm, dk_hbm, dv_hbm, dg_hbm, dk, dv, sem
):
    copies = [
        pltpu.make_async_copy(dq_in, dq_hbm, sem.at[0]),
        pltpu.make_async_copy(dg_in, dg_hbm, sem.at[1]),
    ]
    for copy in copies:
        copy.start()
    for h in range(HEADS):
        leaving = ent[h].astype(BF16)
        dk[:, lanes(h)] = (dki[:, lanes(h)] + nt(wv[:, lanes(h)], leaving)).astype(BF16)
        dv[:, lanes(h)] = (dvi[:, lanes(h)] + nn(wk[:, lanes(h)], leaving)).astype(BF16)
        for i, (src, dst) in enumerate(((dk, dk_hbm), (dv, dv_hbm))):
            copy = pltpu.make_async_copy(
                src.at[:, lanes(h)], dst.at[:, lanes(h)], sem.at[2 + 2 * h + i]
            )
            copy.start()
            copies.append(copy)
    for copy in copies:
        copy.wait()


def build(nx, nz, nh):
    chips = nx * nz
    rows = HALF * DH // chips
    wide = (BLOCK, HEADS * DH)
    per_head = (HEADS, BLOCK, DH)

    def vmem(shape, dtype=F32):
        return pltpu.VMEM(shape, dtype)

    shards, halves = vmem((chips, rows, DH)), vmem((HALF, chips, rows, DH))
    scratch = (
        [vmem(wide, BF16)] * 5
        + [vmem((HEADS, BLOCK)), vmem((1, HEADS * DH))]
        + [vmem((3, 8, BLOCK)), vmem((BLOCK, DH)), vmem(per_head)]
        + [vmem((HEADS, DH, BLOCK), BF16)] * 2
        + [vmem(per_head, BF16)]
        + [vmem((HEADS, BLOCK, BLOCK)), vmem((HEADS, BLOCK, BLOCK), BF16)]
        + [vmem(wide)] * 3
        + [vmem(wide, BF16)]
        + [vmem((8, DH))] * 2
        + [vmem((chips, 8, DH))] * 2
        + [halves, shards, shards, shards, shards, halves, shards, shards]
        + [halves, shards, shards, shards, shards, shards, shards]
        + [vmem((8, DH)), vmem((nh, 8, DH))]
        + [pltpu.SemaphoreType.DMA((7,))]
        + [pltpu.SemaphoreType.DMA((12,))] * 2
    )
    any_space = pl.BlockSpec(memory_space=pl.ANY)
    in_vmem = pl.BlockSpec(memory_space=pltpu.VMEM)

    def local(q, k, v, gate, gout, log_decay, gain):
        made = pl.pallas_call(
            functools.partial(kernel, nx, nz, nh),
            out_shape=[kept(wide, BF16)] * 2
            + [kept(wide, F32)] * 2
            + [kept(wide, BF16)] * 2
            + [kept((HALF, chips, rows, DH), F32)],
            in_specs=[any_space] * 7,
            out_specs=[in_vmem] * 7,
            scratch_shapes=scratch,
            compiler_params=pltpu.CompilerParams(
                collective_id=0, has_side_effects=True, vmem_limit_bytes=36 * 2**20
            ),
        )(*placed(
            (q, k, v, gate, gout, log_decay.T, gain.reshape(1, HEADS * DH)), pltpu.HBM
        ))
        made = list(made)
        made[-1] = made[-1].reshape(HEADS, DH, DH)
        return tuple(
            pl.pallas_call(
                finish,
                out_shape=[jax.ShapeDtypeStruct(wide, BF16)] * 4,
                in_specs=[in_vmem] * 7,
                out_specs=[any_space] * 4,
                scratch_shapes=[vmem(wide, BF16)] * 2 + [pltpu.SemaphoreType.DMA((10,))],
                compiler_params=pltpu.CompilerParams(vmem_limit_bytes=8 * 2**20),
            )(*placed(made, pltpu.VMEM))
        )

    return local


def solution(mesh):
    nx, nz = NX, NZ
    if mesh.shape["ctx"] != 2 * nx * nz:
        nx = nz = 2
    part = P("ctx", "head")
    return jax.shard_map(
        build(nx, nz, mesh.shape["head"]),
        mesh=mesh,
        in_specs=(part,) * 6 + (P("head"),),
        out_specs=(part,) * 4,
        check_vma=False,
    )
```

```python
import functools

import jax
import jax.numpy as jnp
from jax import lax
from jax.experimental import pallas as pl
from jax.experimental.pallas import tpu as pltpu
from jax.sharding import PartitionSpec as P

BLOCK = 512
DH = 128
HEADS = 4
HALF = HEADS // 2
TILE = 256
NX = 4
NZ = 8
F32 = jnp.float32
BF16 = jnp.bfloat16
MESH = pl.DeviceIdType.MESH


def nn(a, b):
    return jnp.dot(a, b, preferred_element_type=F32)


def nt(a, b):
    return lax.dot_general(a, b, (((1,), (1,)), ((), ())), preferred_element_type=F32)


def lane_cumsum(x):
    place = lax.broadcasted_iota(jnp.int32, x.shape, 1)
    step = 1
    while step < x.shape[1]:
        x = x + jnp.where(place >= step, pltpu.roll(x, step, 1), 0.0)
        step *= 2
    return x


def turned(rows):
    pad = jnp.zeros((DH - rows.shape[0], rows.shape[1]), F32)
    return jnp.concatenate([rows, pad], axis=0).T


def kept(shape, dtype):
    return pltpu.VMEM(shape, dtype)


def placed(values, space):
    return [pltpu.with_memory_space_constraint(value, space) for value in values]


def lanes(h):
    return slice(h * DH, (h + 1) * DH)


def kernel(
    nx, nz, nh,
    q_hbm, k_hbm, v_hbm, gate_hbm, gout_hbm, ld_hbm, gain_hbm,
    dq, dg, dki, dvi, wk, wv, r_ent,
    q, k, v, gate, gout, ld, gain,
    row_form, col_form, ea_col,
    qt, wqt, wq, mask, fw, att, gn, gg, gb,
    g_own, g_par, g_all, decay,
    f_own, f_par, f_chip, f_zin, f_back, f_ent, f_pair, f_pre,
    r_own, r_par, r_chip, r_zin, r_back, r_pair, r_pre,
    y_out, y_in,
    local_sem, send_sem, recv_sem,
):
    me, head = lax.axis_index("ctx"), lax.axis_index("head")
    core, chip_at = me % 2, me // 2
    z, x = chip_at % nz, chip_at // nz
    chips = nx * nz
    rows = HALF * DH // chips
    per_head = chips // HALF

    def at(xx, zz, cc):
        return ((xx * nz + zz) * 2 + cc, head)

    partner = at(x, z, 1 - core)
    sign = 1 - 2 * core

    def shifted(place, d, n):
        return (place + n + sign * d) % n

    def outward(n):
        return sorted(range(n), key=lambda d: -min(d, n - d))

    steps = [(dx, dz) for dx in outward(nx) for dz in outward(nz) if (dx, dz) != (0, 0)]
    others = [(shifted(x, dx, nx), shifted(z, dz, nz)) for dx, dz in steps]
    z_peers = [at(x, (z + d) % nz, core) for d in range(1, nz)]
    x_peers = [at((x + d) % nx, z, core) for d in range(1, nx)]
    chip_peers = [at(xx, zz, core) for xx, zz in others]
    y_peers = [(me, shifted(head, d, nh)) for d in outward(nh) if d]

    loads = {}
    for i, (name, src, dst) in enumerate((
        ("ld", ld_hbm, ld), ("k", k_hbm, k), ("v", v_hbm, v), ("q", q_hbm, q),
        ("gate", gate_hbm, gate), ("gout", gout_hbm, gout), ("gain", gain_hbm, gain),
    )):
        loads[name] = pltpu.make_async_copy(src, dst, local_sem.at[i])
        loads[name].start()
    barrier = pltpu.get_barrier_semaphore()
    peers = [partner] + chip_peers + y_peers
    for peer in peers:
        pl.semaphore_signal(barrier, inc=1, device_id=peer, device_id_type=MESH)

    sent = []
    used = [0]

    def fresh(n=1):
        used[0] += n
        return used[0] - n

    def start(src, dst, device, send_at, recv_at):
        pltpu.make_async_remote_copy(
            src_ref=src, dst_ref=dst, send_sem=send_sem.at[send_at],
            recv_sem=recv_sem.at[recv_at], device_id=device, device_id_type=MESH,
        ).start()

    def send(copies, span):
        mine = fresh()
        for src, dst, device in copies:
            start(src, dst, device, mine, mine)
        sent.append((mine, span))
        return mine, span

    def arrived(handle):
        mine, span = handle
        pltpu.make_async_copy(span, span, recv_sem.at[mine]).wait()

    def first(reverse):
        return (core == 1) if reverse else (core == 0)

    def decay_row(ref, i):
        return jnp.exp(ref[pl.ds(HALF * core + i, 1), :])

    def part(i):
        return slice(i * per_head, (i + 1) * per_head)

    parity = z % 2
    my_shard = parity * per_head + chip_at // 2
    pairs = nz // 2

    def stage_pair(own, par, i):
        here = pl.ds(i * per_head, per_head)
        return send([(own.at[1 - core, here], par.at[here], partner)], par.at[here])

    def stage_chip(own, par, chip, zin, i, sems, reverse):
        one = jnp.ones((1, DH), F32)
        w_own = jnp.where(first(reverse), decay_row(g_par, i), one)
        w_par = jnp.where(first(reverse), one, decay_row(g_own, i))
        chip[part(i)] = w_own * own[core, part(i)] + w_par * par[part(i)]

        def post(xx, zz):
            shard = i * per_head + (xx * nz + zz) // 2
            start(chip.at[shard], zin.at[chip_at], at(xx, zz, core), sems, sems)

        for dx in outward(nx):
            for p in outward(pairs):
                if p or dx:
                    post(shifted(x, dx, nx), 2 * shifted(z // 2, p, pairs) + i)

        @pl.when(parity != i)
        def _():
            post(x, 2 * (z // 2) + i)

        @pl.when(parity == i)
        def _():
            zin[chip_at] = chip[my_shard]

    def stage_fold(zin, pre, back, sems, reverse):
        all_others = zin.at[pl.ds(0, chips - 1)]
        arrived((sems, all_others))
        sent.append((sems, all_others))
        total = jnp.zeros((rows, DH), F32)
        for j in reversed(range(chips)) if reverse else range(chips):
            pre[j] = total
            total = decay[j, 0:1, :] * total + zin[j]
        mine = fresh(2)
        for (xx, zz), device in zip(others, chip_peers):
            start(pre.at[xx * nz + zz], back.at[my_shard], device, mine, mine + parity)
        sent.append((mine, all_others))
        back[my_shard] = pre[chip_at]
        return mine

    def stage_split(own, par, back, ent, pair, i, sems, reverse):
        @pl.when(parity != i)
        def _():
            arrived((sems + i, back.at[pl.ds(0, per_head)]))

        @pl.when(parity == i)
        def _():
            arrived((sems + i, back.at[pl.ds(0, per_head - 1)]))

        one, zero = jnp.ones((1, DH), F32), jnp.zeros((1, DH), F32)
        lead = first(reverse)
        here = pl.ds(i * per_head, per_head)
        w_par = jnp.where(lead, decay_row(g_own, i), one)
        s_par = jnp.where(lead, one, zero)
        pair[part(i)] = w_par * back[part(i)] + s_par * own[core, part(i)]
        handle = send([(pair.at[here], ent.at[core, here], partner)], pair.at[here])
        w_own = jnp.where(lead, one, decay_row(g_par, i))
        s_own = jnp.where(lead, zero, one)
        ent[core, part(i)] = w_own * back[part(i)] + s_own * par[part(i)]
        return handle

    def state_b(ent, h):
        return ent[h // HALF, part(h % HALF)].reshape(DH, DH).astype(BF16)

    loads["ld"].wait()
    cumul = lane_cumsum(jnp.concatenate([ld[...], ld[...]], axis=0))
    total = cumul[:, BLOCK - 1 :]
    g_own[...] = jnp.broadcast_to(total, (8, DH))
    ea, tail = jnp.exp(cumul), jnp.exp(total - cumul)
    row_form[0], row_form[1], row_form[2] = cumul, ea, tail
    loads["k"].wait()
    loads["v"].wait()
    f_copies = []
    for i in range(HALF):
        for h in (i, HALF + i):
            weighted = (k[:, lanes(h)].T.astype(F32) * tail[h : h + 1, :]).astype(BF16)
            f_own[h // HALF, part(i)] = nn(weighted, v[:, lanes(h)]).reshape(
                per_head, rows, DH
            )
        if i == 0:
            pl.semaphore_wait(barrier, len(peers))
            g_copies = send([(g_own, g_par, partner)], g_par)
        f_copies.append(stage_pair(f_own, f_par, i))

    def column(kind, h):
        j = 8 * kind + h
        return jnp.broadcast_to(col_form[:, j : j + 1], (BLOCK, DH))

    def prepare(h):
        ea_here = column(1, h)
        tail_here = column(2, h)
        ea_col[h] = ea_here
        q_here = q[:, lanes(h)]
        wq[h] = (q_here.astype(F32) * ea_here).astype(BF16)
        wk[:, lanes(h)] = (k[:, lanes(h)].astype(F32) * tail_here).astype(BF16)
        wv[:, lanes(h)] = (v[:, lanes(h)].astype(F32) * tail_here).astype(BF16)
        turned_q = q_here.T
        qt[h] = turned_q
        wqt[h] = (turned_q.astype(F32) * row_form[1, h : h + 1, :]).astype(BF16)

    def intra(h):
        a_here = row_form[0, h : h + 1, :]
        a_col = column(0, h)
        for t in range(0, BLOCK, TILE):
            seen = t + TILE
            here = slice(t, seen)
            scores = nt(q[here, lanes(h)], k[:seen, lanes(h)])
            col = jnp.concatenate([a_col[here]] * (seen // DH), axis=1)
            diff = col - a_here[:, :seen]
            keep = lax.broadcasted_iota(jnp.int32, diff.shape, 0) + t >= (
                lax.broadcasted_iota(jnp.int32, diff.shape, 1)
            )
            weight = jnp.where(keep, jnp.exp(jnp.where(keep, diff, 0.0)), 0.0)
            mask[h, here, :seen] = weight
            weights = (scores * weight).astype(BF16)
            fw[h, here, :seen] = weights
            att[here, lanes(h)] = nn(weights, v[:seen, lanes(h)])

    def gates(h):
        sig = jax.nn.sigmoid(gate[:, lanes(h)].astype(F32))
        normed = gout[:, lanes(h)].astype(F32) * sig * gain[:, lanes(h)]
        gn[:, lanes(h)] = normed
        gg[:, lanes(h)] = normed * (1.0 - sig)

    arrived(g_copies)
    g_all[chip_at] = g_own[...] + g_par[...]
    g_copies = send(
        [(g_all.at[chip_at], g_all.at[chip_at], peer) for peer in z_peers],
        g_all.at[pl.ds(0, nz - 1)],
    )
    f_sems = fresh()
    for i in range(HALF):
        arrived(f_copies[i])
        stage_chip(f_own, f_par, f_chip, f_zin, i, f_sems, False)
    col_form[...] = turned(jnp.concatenate([cumul, ea, tail], axis=0))
    loads["q"].wait()
    prepare(0)
    arrived(g_copies)
    row_at = pl.ds(x * nz, nz)
    g_copies = send(
        [(g_all.at[row_at], g_all.at[row_at], peer) for peer in x_peers],
        g_all.at[pl.ds(0, nz * (nx - 1))],
    )
    intra(0)
    prepare(1)
    intra(1)
    arrived(g_copies)
    for j in range(chips):
        decay[j] = jnp.broadcast_to(
            jnp.exp(g_all[j, pl.ds(HALF * core + parity, 1), :]), (8, DH)
        )
    f_sems = stage_fold(f_zin, f_pre, f_back, f_sems, False)
    for h in range(2, HEADS):
        prepare(h)
        intra(h)
    for name in ("gate", "gout", "gain"):
        loads[name].wait()
    for h in range(HEADS):
        gates(h)
    f_copies = [
        stage_split(f_own, f_par, f_back, f_ent, f_pair, i, f_sems, False)
        for i in range(HALF)
    ]

    squares = jnp.zeros((BLOCK, DH), F32)
    inner = jnp.zeros((BLOCK, DH), F32)
    for i in range(HALF):
        arrived(f_copies[i])
        for h in (i, HALF + i):
            full = att[:, lanes(h)] + nn(wq[h], state_b(f_ent, h))
            att[:, lanes(h)] = full
            squares = squares + full * full
            inner = inner + full * gn[:, lanes(h)]

    ones = jnp.ones((8, DH), BF16)

    def row_sums(value):
        high = value.astype(BF16)
        low = (value - high.astype(F32)).astype(BF16)
        return nt(ones, high) + nt(ones, low)

    sums = [row_sums(squares), row_sums(inner)]
    parts = BLOCK // DH
    y_out[...] = jnp.concatenate(
        [s[0:1, i * DH : (i + 1) * DH] for s in sums for i in range(parts)], axis=0
    )
    copies = send(
        [(y_out, y_in.at[head], peer) for peer in y_peers], y_in.at[pl.ds(0, nh - 1)]
    )
    y_in[head] = y_out[...]
    arrived(copies)
    summed = y_in[0]
    for i in range(1, nh):
        summed = summed + y_in[i]
    features = HEADS * DH * nh
    rms = lax.rsqrt(summed[:parts] / features + 1e-05)
    coef = rms * rms * rms * summed[parts:] / features
    scales = turned(jnp.concatenate([rms, coef], axis=0))

    def scale_column(first_lane):
        return jnp.concatenate(
            [
                jnp.broadcast_to(scales[:, i : i + 1], (DH, DH))
                for i in range(first_lane, first_lane + parts)
            ],
            axis=0,
        )

    rms_col, coef_col = scale_column(0), scale_column(parts)
    r_copies = []
    for i in range(HALF):
        for h in (i, HALF + i):
            grad = (rms_col * gn[:, lanes(h)] - att[:, lanes(h)] * coef_col).astype(BF16)
            gb[:, lanes(h)] = grad
            r_own[h // HALF, part(i)] = nn(wqt[h], grad).reshape(per_head, rows, DH)
        r_copies.append(stage_pair(r_own, r_par, i))

    def back(h):
        grad = gb[:, lanes(h)]
        entering = state_b(f_ent, h)
        upper = []
        for t in range(0, BLOCK, TILE):
            seen = t + TILE
            here = slice(t, seen)
            weights = (nt(grad[here], v[:seen, lanes(h)]) * mask[h, here, :seen]).astype(BF16)
            upper.append(weights)
            dq[here, lanes(h)] = (
                nn(weights, k[:seen, lanes(h)]) + ea_col[h, here, :] * nt(grad[here], entering)
            ).astype(BF16)
        gt = grad.T
        for s in range(0, BLOCK, TILE):
            here = slice(s, s + TILE)
            key = value = None
            for t in range(s, BLOCK, TILE):
                there = slice(t, t + TILE)
                one_key = nn(qt[h, :, there], upper[t // TILE][:, here])
                one_value = nn(gt[:, there], fw[h, there, here])
                key = one_key if key is None else key + one_key
                value = one_value if value is None else value + one_value
            dki[here, lanes(h)] = key.T
            dvi[here, lanes(h)] = value.T

    for h in range(HEADS):
        dg[:, lanes(h)] = (gg[:, lanes(h)] * att[:, lanes(h)] * rms_col).astype(BF16)
    r_sems = fresh()
    for i in range(HALF):
        arrived(r_copies[i])
        stage_chip(r_own, r_par, r_chip, r_zin, i, r_sems, True)
    back(0)
    back(1)
    r_sems = stage_fold(r_zin, r_pre, r_back, r_sems, True)
    back(2)
    back(3)
    r_copies = [
        stage_split(r_own, r_par, r_back, r_ent, r_pair, i, r_sems, True)
        for i in range(HALF)
    ]
    for i in range(HALF):
        arrived(r_copies[i])
    for mine, span in sent:
        pltpu.make_async_copy(span, span, send_sem.at[mine]).wait()


def finish(
    dq_in, dg_in, dki, dvi, wk, wv, ent, dq_hbm, dk_hbm, dv_hbm, dg_hbm, dk, dv, sem
):
    copies = [
        pltpu.make_async_copy(dq_in, dq_hbm, sem.at[0]),
        pltpu.make_async_copy(dg_in, dg_hbm, sem.at[1]),
    ]
    for copy in copies:
        copy.start()
    for h in range(HEADS):
        leaving = ent[h].astype(BF16)
        dk[:, lanes(h)] = (dki[:, lanes(h)] + nt(wv[:, lanes(h)], leaving)).astype(BF16)
        dv[:, lanes(h)] = (dvi[:, lanes(h)] + nn(wk[:, lanes(h)], leaving)).astype(BF16)
        for i, (src, dst) in enumerate(((dk, dk_hbm), (dv, dv_hbm))):
            copy = pltpu.make_async_copy(
                src.at[:, lanes(h)], dst.at[:, lanes(h)], sem.at[2 + 2 * h + i]
            )
            copy.start()
            copies.append(copy)
    for copy in copies:
        copy.wait()


def build(nx, nz, nh):
    chips = nx * nz
    rows = HALF * DH // chips
    wide = (BLOCK, HEADS * DH)
    per_head = (HEADS, BLOCK, DH)

    def vmem(shape, dtype=F32):
        return pltpu.VMEM(shape, dtype)

    shards, halves = vmem((chips, rows, DH)), vmem((HALF, chips, rows, DH))
    scratch = (
        [vmem(wide, BF16)] * 5
        + [vmem((HEADS, BLOCK)), vmem((1, HEADS * DH))]
        + [vmem((3, 8, BLOCK)), vmem((BLOCK, DH)), vmem(per_head)]
        + [vmem((HEADS, DH, BLOCK), BF16)] * 2
        + [vmem(per_head, BF16)]
        + [vmem((HEADS, BLOCK, BLOCK)), vmem((HEADS, BLOCK, BLOCK), BF16)]
        + [vmem(wide)] * 3
        + [vmem(wide, BF16)]
        + [vmem((8, DH))] * 2
        + [vmem((chips, 8, DH))] * 2
        + [halves, shards, shards, shards, shards, halves, shards, shards]
        + [halves, shards, shards, shards, shards, shards, shards]
        + [vmem((8, DH)), vmem((nh, 8, DH))]
        + [pltpu.SemaphoreType.DMA((7,))]
        + [pltpu.SemaphoreType.DMA((18,))] * 2
    )
    any_space = pl.BlockSpec(memory_space=pl.ANY)
    in_vmem = pl.BlockSpec(memory_space=pltpu.VMEM)

    def local(q, k, v, gate, gout, log_decay, gain):
        made = pl.pallas_call(
            functools.partial(kernel, nx, nz, nh),
            out_shape=[kept(wide, BF16)] * 2
            + [kept(wide, F32)] * 2
            + [kept(wide, BF16)] * 2
            + [kept((HALF, chips, rows, DH), F32)],
            in_specs=[any_space] * 7,
            out_specs=[in_vmem] * 7,
            scratch_shapes=scratch,
            compiler_params=pltpu.CompilerParams(
                collective_id=0, has_side_effects=True, vmem_limit_bytes=36 * 2**20
            ),
        )(*placed(
            (q, k, v, gate, gout, log_decay.T, gain.reshape(1, HEADS * DH)), pltpu.HBM
        ))
        made = list(made)
        made[-1] = made[-1].reshape(HEADS, DH, DH)
        return tuple(
            pl.pallas_call(
                finish,
                out_shape=[jax.ShapeDtypeStruct(wide, BF16)] * 4,
                in_specs=[in_vmem] * 7,
                out_specs=[any_space] * 4,
                scratch_shapes=[vmem(wide, BF16)] * 2 + [pltpu.SemaphoreType.DMA((10,))],
                compiler_params=pltpu.CompilerParams(vmem_limit_bytes=8 * 2**20),
            )(*placed(made, pltpu.VMEM))
        )

    return local


def solution(mesh):
    nx, nz = NX, NZ
    if mesh.shape["ctx"] != 2 * nx * nz:
        nx = nz = 2
    part = P("ctx", "head")
    return jax.shard_map(
        build(nx, nz, mesh.shape["head"]),
        mesh=mesh,
        in_specs=(part,) * 6 + (P("head"),),
        out_specs=(part,) * 4,
        check_vma=False,
    )
```

```python
import functools

import jax
import jax.numpy as jnp
from jax import lax
from jax.experimental import pallas as pl
from jax.experimental.pallas import tpu as pltpu
from jax.sharding import PartitionSpec as P

BLOCK = 512
DH = 128
HEADS = 4
HALF = HEADS // 2
TILE = 256
NX = 4
NZ = 8
F32 = jnp.float32
BF16 = jnp.bfloat16
MESH = pl.DeviceIdType.MESH


def nn(a, b):
    return jnp.dot(a, b, preferred_element_type=F32)


def nt(a, b):
    return lax.dot_general(a, b, (((1,), (1,)), ((), ())), preferred_element_type=F32)


def lane_cumsum(x):
    place = lax.broadcasted_iota(jnp.int32, x.shape, 1)
    step = 1
    while step < x.shape[1]:
        x = x + jnp.where(place >= step, pltpu.roll(x, step, 1), 0.0)
        step *= 2
    return x


def turned(rows):
    pad = jnp.zeros((DH - rows.shape[0], rows.shape[1]), F32)
    return jnp.concatenate([rows, pad], axis=0).T


def kept(shape, dtype):
    return pltpu.VMEM(shape, dtype)


def placed(values, space):
    return [pltpu.with_memory_space_constraint(value, space) for value in values]


def lanes(h):
    return pl.ds(h * DH if isinstance(h, int) else pl.multiple_of(h * DH, DH), DH)


def kernel(
    nx, nz, nh,
    q_hbm, k_hbm, v_hbm, gate_hbm, gout_hbm, ld_hbm, gain_hbm,
    dq, dg, dki, dvi, wk, wv, r_ent,
    q, k, v, gate, gout, ld, gain,
    row_form, col_form, ea_col,
    qt, wqt, wq, mask, fw, att, gn, gg, gb,
    g_own, g_par, g_all, decay,
    f_own, f_par, f_chip, f_zin, f_back, f_ent, f_pair, f_pre,
    r_own, r_par, r_chip, r_zin, r_back, r_pair, r_pre,
    y_out, y_in,
    local_sem, send_sem, recv_sem,
):
    me, head = lax.axis_index("ctx"), lax.axis_index("head")
    core, chip_at = me % 2, me // 2
    z, x = chip_at % nz, chip_at // nz
    chips = nx * nz
    rows = HALF * DH // chips
    per_head = chips // HALF

    def at(xx, zz, cc):
        return ((xx * nz + zz) * 2 + cc, head)

    partner = at(x, z, 1 - core)
    sign = 1 - 2 * core

    def shifted(place, d, n):
        return (place + n + sign * d) % n

    def outward(n):
        return sorted(range(n), key=lambda d: -min(d, n - d))

    steps = [(dx, dz) for dx in outward(nx) for dz in outward(nz) if (dx, dz) != (0, 0)]
    others = [(shifted(x, dx, nx), shifted(z, dz, nz)) for dx, dz in steps]
    z_peers = [at(x, (z + d) % nz, core) for d in range(1, nz)]
    x_peers = [at((x + d) % nx, z, core) for d in range(1, nx)]
    chip_peers = [at(xx, zz, core) for xx, zz in others]
    y_peers = [(me, shifted(head, d, nh)) for d in outward(nh) if d]

    loads = {}
    for i, (name, src, dst) in enumerate((
        ("ld", ld_hbm, ld), ("k", k_hbm, k), ("v", v_hbm, v), ("q", q_hbm, q),
        ("gate", gate_hbm, gate), ("gout", gout_hbm, gout), ("gain", gain_hbm, gain),
    )):
        loads[name] = pltpu.make_async_copy(src, dst, local_sem.at[i])
        loads[name].start()
    barrier = pltpu.get_barrier_semaphore()
    peers = [partner] + chip_peers + y_peers
    for peer in peers:
        pl.semaphore_signal(barrier, inc=1, device_id=peer, device_id_type=MESH)

    sent = []
    used = [0]

    def fresh(n=1):
        used[0] += n
        return used[0] - n

    def start(src, dst, device, send_at, recv_at):
        pltpu.make_async_remote_copy(
            src_ref=src, dst_ref=dst, send_sem=send_sem.at[send_at],
            recv_sem=recv_sem.at[recv_at], device_id=device, device_id_type=MESH,
        ).start()

    def send(copies, span):
        mine = fresh()
        for src, dst, device in copies:
            start(src, dst, device, mine, mine)
        sent.append((mine, span))
        return mine, span

    def arrived(handle):
        mine, span = handle
        pltpu.make_async_copy(span, span, recv_sem.at[mine]).wait()

    def first(reverse):
        return (core == 1) if reverse else (core == 0)

    def decay_row(ref, i):
        return jnp.exp(ref[pl.ds(HALF * core + i, 1), :])

    def part(i):
        return slice(i * per_head, (i + 1) * per_head)

    parity = z % 2
    my_shard = parity * per_head + chip_at // 2
    pairs = nz // 2

    def stage_pair(own, par, i):
        here = pl.ds(i * per_head, per_head)
        return send([(own.at[1 - core, here], par.at[here], partner)], par.at[here])

    def stage_chip(own, par, chip, zin, i, sems, reverse):
        one = jnp.ones((1, DH), F32)
        w_own = jnp.where(first(reverse), decay_row(g_par, i), one)
        w_par = jnp.where(first(reverse), one, decay_row(g_own, i))
        chip[part(i)] = w_own * own[core, part(i)] + w_par * par[part(i)]

        def post(xx, zz):
            shard = i * per_head + (xx * nz + zz) // 2
            start(chip.at[shard], zin.at[chip_at], at(xx, zz, core), sems, sems)

        for dx in outward(nx):
            for p in outward(pairs):
                if p or dx:
                    post(shifted(x, dx, nx), 2 * shifted(z // 2, p, pairs) + i)

        @pl.when(parity != i)
        def _():
            post(x, 2 * (z // 2) + i)

        @pl.when(parity == i)
        def _():
            zin[chip_at] = chip[my_shard]

    def stage_fold(zin, pre, back, sems, reverse):
        all_others = zin.at[pl.ds(0, chips - 1)]
        arrived((sems, all_others))
        sent.append((sems, all_others))
        total = jnp.zeros((rows, DH), F32)
        for j in reversed(range(chips)) if reverse else range(chips):
            pre[j] = total
            total = decay[j, 0:1, :] * total + zin[j]
        mine = fresh(2)
        for (xx, zz), device in zip(others, chip_peers):
            start(pre.at[xx * nz + zz], back.at[my_shard], device, mine, mine + parity)
        sent.append((mine, all_others))
        back[my_shard] = pre[chip_at]
        return mine

    def stage_split(own, par, back, ent, pair, i, sems, reverse):
        @pl.when(parity != i)
        def _():
            arrived((sems + i, back.at[pl.ds(0, per_head)]))

        @pl.when(parity == i)
        def _():
            arrived((sems + i, back.at[pl.ds(0, per_head - 1)]))

        one, zero = jnp.ones((1, DH), F32), jnp.zeros((1, DH), F32)
        lead = first(reverse)
        here = pl.ds(i * per_head, per_head)
        w_par = jnp.where(lead, decay_row(g_own, i), one)
        s_par = jnp.where(lead, one, zero)
        pair[part(i)] = w_par * back[part(i)] + s_par * own[core, part(i)]
        handle = send([(pair.at[here], ent.at[core, here], partner)], pair.at[here])
        w_own = jnp.where(lead, one, decay_row(g_par, i))
        s_own = jnp.where(lead, zero, one)
        ent[core, part(i)] = w_own * back[part(i)] + s_own * par[part(i)]
        return handle

    def state_b(ent, half, i):
        return ent[half, part(i)].reshape(DH, DH).astype(BF16)

    loads["ld"].wait()
    cumul = lane_cumsum(jnp.concatenate([ld[...], ld[...]], axis=0))
    total = cumul[:, BLOCK - 1 :]
    g_own[...] = jnp.broadcast_to(total, (8, DH))
    ea, tail = jnp.exp(cumul), jnp.exp(total - cumul)
    row_form[0], row_form[1], row_form[2] = cumul, ea, tail
    loads["k"].wait()
    loads["v"].wait()
    def block_state(half, i):
        h = HALF * half + i
        weighted = (k[:, lanes(h)].T.astype(F32) * row_form[2, pl.ds(h, 1), :]).astype(BF16)
        f_own[half, part(i)] = nn(weighted, v[:, lanes(h)]).reshape(per_head, rows, DH)

    f_copies = []
    for i in range(HALF):
        block_state(1 - core, i)
        if i == 0:
            pl.semaphore_wait(barrier, len(peers))
            g_copies = send([(g_own, g_par, partner)], g_par)
        f_copies.append(stage_pair(f_own, f_par, i))
    for i in range(HALF):
        block_state(core, i)

    def column(kind, h):
        j = 8 * kind + h
        return jnp.broadcast_to(col_form[:, j : j + 1], (BLOCK, DH))

    def prepare(h):
        ea_here = column(1, h)
        tail_here = column(2, h)
        ea_col[h] = ea_here
        q_here = q[:, lanes(h)]
        wq[h] = (q_here.astype(F32) * ea_here).astype(BF16)
        wk[:, lanes(h)] = (k[:, lanes(h)].astype(F32) * tail_here).astype(BF16)
        wv[:, lanes(h)] = (v[:, lanes(h)].astype(F32) * tail_here).astype(BF16)
        turned_q = q_here.T
        qt[h] = turned_q
        wqt[h] = (turned_q.astype(F32) * row_form[1, h : h + 1, :]).astype(BF16)

    def intra(h):
        a_here = row_form[0, h : h + 1, :]
        a_col = column(0, h)
        for t in range(0, BLOCK, TILE):
            seen = t + TILE
            here = slice(t, seen)
            scores = nt(q[here, lanes(h)], k[:seen, lanes(h)])
            col = jnp.concatenate([a_col[here]] * (seen // DH), axis=1)
            diff = col - a_here[:, :seen]
            keep = lax.broadcasted_iota(jnp.int32, diff.shape, 0) + t >= (
                lax.broadcasted_iota(jnp.int32, diff.shape, 1)
            )
            weight = jnp.where(keep, jnp.exp(jnp.where(keep, diff, 0.0)), 0.0)
            mask[h, here, :seen] = weight
            weights = (scores * weight).astype(BF16)
            fw[h, here, :seen] = weights
            att[here, lanes(h)] = nn(weights, v[:seen, lanes(h)])

    def gates(h):
        sig = jax.nn.sigmoid(gate[:, lanes(h)].astype(F32))
        normed = gout[:, lanes(h)].astype(F32) * sig * gain[:, lanes(h)]
        gn[:, lanes(h)] = normed
        gg[:, lanes(h)] = normed * (1.0 - sig)

    col_form[...] = turned(jnp.concatenate([cumul, ea, tail], axis=0))
    arrived(g_copies)
    g_all[chip_at] = g_own[...] + g_par[...]
    g_copies = send(
        [(g_all.at[chip_at], g_all.at[chip_at], peer) for peer in z_peers],
        g_all.at[pl.ds(0, nz - 1)],
    )
    loads["q"].wait()
    prepare(0)
    f_sems = fresh()
    for i in range(HALF):
        arrived(f_copies[i])
        stage_chip(f_own, f_par, f_chip, f_zin, i, f_sems, False)
    prepare(1)
    arrived(g_copies)
    row_at = pl.ds(x * nz, nz)
    g_copies = send(
        [(g_all.at[row_at], g_all.at[row_at], peer) for peer in x_peers],
        g_all.at[pl.ds(0, nz * (nx - 1))],
    )
    intra(0)
    intra(1)
    arrived(g_copies)
    for j in range(chips):
        decay[j] = jnp.broadcast_to(
            jnp.exp(g_all[j, pl.ds(HALF * core + parity, 1), :]), (8, DH)
        )
    f_sems = stage_fold(f_zin, f_pre, f_back, f_sems, False)
    for h in range(2, HEADS):
        prepare(h)
        intra(h)
    for name in ("gate", "gout", "gain"):
        loads[name].wait()
    for h in range(HEADS):
        gates(h)
    f_copies = [
        stage_split(f_own, f_par, f_back, f_ent, f_pair, i, f_sems, False)
        for i in range(HALF)
    ]

    squares = jnp.zeros((BLOCK, DH), F32)
    inner = jnp.zeros((BLOCK, DH), F32)
    for half in (core, 1 - core):
        for i in range(HALF):
            if half is not core:
                arrived(f_copies[i])
            h = HALF * half + i
            full = att[:, lanes(h)] + nn(wq[h], state_b(f_ent, half, i))
            att[:, lanes(h)] = full
            squares = squares + full * full
            inner = inner + full * gn[:, lanes(h)]

    ones = jnp.ones((8, DH), BF16)

    def row_sums(value):
        high = value.astype(BF16)
        low = (value - high.astype(F32)).astype(BF16)
        return nt(ones, high) + nt(ones, low)

    sums = [row_sums(squares), row_sums(inner)]
    parts = BLOCK // DH
    y_out[...] = jnp.concatenate(
        [s[0:1, i * DH : (i + 1) * DH] for s in sums for i in range(parts)], axis=0
    )
    copies = send(
        [(y_out, y_in.at[head], peer) for peer in y_peers], y_in.at[pl.ds(0, nh - 1)]
    )
    y_in[head] = y_out[...]
    arrived(copies)
    summed = y_in[0]
    for i in range(1, nh):
        summed = summed + y_in[i]
    features = HEADS * DH * nh
    rms = lax.rsqrt(summed[:parts] / features + 1e-05)
    coef = rms * rms * rms * summed[parts:] / features
    scales = turned(jnp.concatenate([rms, coef], axis=0))

    def scale_column(first_lane):
        return jnp.concatenate(
            [
                jnp.broadcast_to(scales[:, i : i + 1], (DH, DH))
                for i in range(first_lane, first_lane + parts)
            ],
            axis=0,
        )

    rms_col, coef_col = scale_column(0), scale_column(parts)
    r_copies = []
    for half in (1 - core, core):
        for i in range(HALF):
            h = HALF * half + i
            grad = (rms_col * gn[:, lanes(h)] - att[:, lanes(h)] * coef_col).astype(BF16)
            gb[:, lanes(h)] = grad
            r_own[half, part(i)] = nn(wqt[h], grad).reshape(per_head, rows, DH)
            if half is not core:
                r_copies.append(stage_pair(r_own, r_par, i))

    def back(h):
        grad = gb[:, lanes(h)]
        entering = state_b(f_ent, h // HALF, h % HALF)
        upper = []
        for t in range(0, BLOCK, TILE):
            seen = t + TILE
            here = slice(t, seen)
            weights = (nt(grad[here], v[:seen, lanes(h)]) * mask[h, here, :seen]).astype(BF16)
            upper.append(weights)
            dq[here, lanes(h)] = (
                nn(weights, k[:seen, lanes(h)]) + ea_col[h, here, :] * nt(grad[here], entering)
            ).astype(BF16)
        gt = grad.T
        for s in range(0, BLOCK, TILE):
            here = slice(s, s + TILE)
            key = value = None
            for t in range(s, BLOCK, TILE):
                there = slice(t, t + TILE)
                one_key = nn(qt[h, :, there], upper[t // TILE][:, here])
                one_value = nn(gt[:, there], fw[h, there, here])
                key = one_key if key is None else key + one_key
                value = one_value if value is None else value + one_value
            dki[here, lanes(h)] = key.T
            dvi[here, lanes(h)] = value.T

    for h in range(HEADS):
        dg[:, lanes(h)] = (gg[:, lanes(h)] * att[:, lanes(h)] * rms_col).astype(BF16)
    r_sems = fresh()
    for i in range(HALF):
        arrived(r_copies[i])
        stage_chip(r_own, r_par, r_chip, r_zin, i, r_sems, True)
    back(0)
    back(1)
    r_sems = stage_fold(r_zin, r_pre, r_back, r_sems, True)
    back(2)
    back(3)
    r_copies = [
        stage_split(r_own, r_par, r_back, r_ent, r_pair, i, r_sems, True)
        for i in range(HALF)
    ]
    for i in range(HALF):
        arrived(r_copies[i])
    for mine, span in sent:
        pltpu.make_async_copy(span, span, send_sem.at[mine]).wait()


def finish(
    dq_in, dg_in, dki, dvi, wk, wv, ent, dq_hbm, dk_hbm, dv_hbm, dg_hbm, dk, dv, sem
):
    copies = [
        pltpu.make_async_copy(dq_in, dq_hbm, sem.at[0]),
        pltpu.make_async_copy(dg_in, dg_hbm, sem.at[1]),
    ]
    for copy in copies:
        copy.start()
    for h in range(HEADS):
        leaving = ent[h].astype(BF16)
        dk[:, lanes(h)] = (dki[:, lanes(h)] + nt(wv[:, lanes(h)], leaving)).astype(BF16)
        dv[:, lanes(h)] = (dvi[:, lanes(h)] + nn(wk[:, lanes(h)], leaving)).astype(BF16)
        for i, (src, dst) in enumerate(((dk, dk_hbm), (dv, dv_hbm))):
            copy = pltpu.make_async_copy(
                src.at[:, lanes(h)], dst.at[:, lanes(h)], sem.at[2 + 2 * h + i]
            )
            copy.start()
            copies.append(copy)
    for copy in copies:
        copy.wait()


def build(nx, nz, nh):
    chips = nx * nz
    rows = HALF * DH // chips
    wide = (BLOCK, HEADS * DH)
    per_head = (HEADS, BLOCK, DH)

    def vmem(shape, dtype=F32):
        return pltpu.VMEM(shape, dtype)

    shards, halves = vmem((chips, rows, DH)), vmem((HALF, chips, rows, DH))
    scratch = (
        [vmem(wide, BF16)] * 5
        + [vmem((HEADS, BLOCK)), vmem((1, HEADS * DH))]
        + [vmem((3, 8, BLOCK)), vmem((BLOCK, DH)), vmem(per_head)]
        + [vmem((HEADS, DH, BLOCK), BF16)] * 2
        + [vmem(per_head, BF16)]
        + [vmem((HEADS, BLOCK, BLOCK)), vmem((HEADS, BLOCK, BLOCK), BF16)]
        + [vmem(wide)] * 3
        + [vmem(wide, BF16)]
        + [vmem((8, DH))] * 2
        + [vmem((chips, 8, DH))] * 2
        + [halves, shards, shards, shards, shards, halves, shards, shards]
        + [halves, shards, shards, shards, shards, shards, shards]
        + [vmem((8, DH)), vmem((nh, 8, DH))]
        + [pltpu.SemaphoreType.DMA((7,))]
        + [pltpu.SemaphoreType.DMA((18,))] * 2
    )
    any_space = pl.BlockSpec(memory_space=pl.ANY)
    in_vmem = pl.BlockSpec(memory_space=pltpu.VMEM)

    def local(q, k, v, gate, gout, log_decay, gain):
        made = pl.pallas_call(
            functools.partial(kernel, nx, nz, nh),
            out_shape=[kept(wide, BF16)] * 2
            + [kept(wide, F32)] * 2
            + [kept(wide, BF16)] * 2
            + [kept((HALF, chips, rows, DH), F32)],
            in_specs=[any_space] * 7,
            out_specs=[in_vmem] * 7,
            scratch_shapes=scratch,
            compiler_params=pltpu.CompilerParams(
                collective_id=0, has_side_effects=True, vmem_limit_bytes=36 * 2**20
            ),
        )(*placed(
            (q, k, v, gate, gout, log_decay.T, gain.reshape(1, HEADS * DH)), pltpu.HBM
        ))
        made = list(made)
        made[-1] = made[-1].reshape(HEADS, DH, DH)
        return tuple(
            pl.pallas_call(
                finish,
                out_shape=[jax.ShapeDtypeStruct(wide, BF16)] * 4,
                in_specs=[in_vmem] * 7,
                out_specs=[any_space] * 4,
                scratch_shapes=[vmem(wide, BF16)] * 2 + [pltpu.SemaphoreType.DMA((10,))],
                compiler_params=pltpu.CompilerParams(vmem_limit_bytes=8 * 2**20),
            )(*placed(made, pltpu.VMEM))
        )

    return local


def solution(mesh):
    nx, nz = NX, NZ
    if mesh.shape["ctx"] != 2 * nx * nz:
        nx = nz = 2
    part = P("ctx", "head")
    return jax.shard_map(
        build(nx, nz, mesh.shape["head"]),
        mesh=mesh,
        in_specs=(part,) * 6 + (P("head"),),
        out_specs=(part,) * 4,
        check_vma=False,
    )
```

```python
import functools

import jax
import jax.numpy as jnp
from jax import lax
from jax.experimental import pallas as pl
from jax.experimental.pallas import tpu as pltpu
from jax.sharding import PartitionSpec as P

BLOCK = 512
DH = 128
HEADS = 4
HALF = HEADS // 2
TILE = 256
NX = 4
NZ = 8
F32 = jnp.float32
BF16 = jnp.bfloat16
MESH = pl.DeviceIdType.MESH


def nn(a, b):
    return jnp.dot(a, b, preferred_element_type=F32)


def nt(a, b):
    return lax.dot_general(a, b, (((1,), (1,)), ((), ())), preferred_element_type=F32)


def lane_cumsum(x):
    place = lax.broadcasted_iota(jnp.int32, x.shape, 1)
    step = 1
    while step < x.shape[1]:
        x = x + jnp.where(place >= step, pltpu.roll(x, step, 1), 0.0)
        step *= 2
    return x


def turned(rows):
    pad = jnp.zeros((DH - rows.shape[0], rows.shape[1]), F32)
    return jnp.concatenate([rows, pad], axis=0).T


def kept(shape, dtype):
    return pltpu.VMEM(shape, dtype)


def placed(values, space):
    return [pltpu.with_memory_space_constraint(value, space) for value in values]


def lanes(h):
    return pl.ds(h * DH if isinstance(h, int) else pl.multiple_of(h * DH, DH), DH)


def kernel(
    nx, nz, nh,
    q_hbm, k_hbm, v_hbm, gate_hbm, gout_hbm, ld_hbm, gain_hbm,
    dq, dg, dki, dvi, wk, wv, r_ent,
    q, k, v, gate, gout, ld, gain,
    row_form, col_form, columns,
    qt, wqt, wq, mask, fw, att, gn, gg, gb,
    g_own, g_par, g_all, decay, x_out, x_in, att_par, wqt_par,
    f_own, f_par, f_chip, f_zin, f_back, f_ent, f_pair, f_pre,
    r_own, r_par, r_chip, r_zin, r_back, r_pair, r_pre,
    y_out, y_in,
    local_sem, send_sem, recv_sem,
):
    me, head = lax.axis_index("ctx"), lax.axis_index("head")
    core, chip_at = me % 2, me // 2
    z, x = chip_at % nz, chip_at // nz
    chips = nx * nz
    rows = HALF * DH // chips
    per_head = chips // HALF

    def at(xx, zz, cc):
        return ((xx * nz + zz) * 2 + cc, head)

    partner = at(x, z, 1 - core)
    sign = 1 - 2 * core

    def shifted(place, d, n):
        return (place + n + sign * d) % n

    def outward(n):
        return sorted(range(n), key=lambda d: -min(d, n - d))

    steps = [(dx, dz) for dx in outward(nx) for dz in outward(nz) if (dx, dz) != (0, 0)]
    others = [(shifted(x, dx, nx), shifted(z, dz, nz)) for dx, dz in steps]
    z_peers = [at(x, (z + d) % nz, core) for d in range(1, nz)]
    x_peers = [at((x + d) % nx, z, core) for d in range(1, nx)]
    chip_peers = [at(xx, zz, core) for xx, zz in others]
    y_peers = [
        (at(x, z, c)[0], shifted(head, d, nh))
        for d in outward(nh)
        for c in (core, 1 - core)
        if d
    ]

    loads = {}
    for i, (name, src, dst) in enumerate((
        ("ld", ld_hbm, ld), ("k", k_hbm, k), ("v", v_hbm, v), ("q", q_hbm, q),
        ("gate", gate_hbm, gate), ("gout", gout_hbm, gout), ("gain", gain_hbm, gain),
    )):
        loads[name] = pltpu.make_async_copy(src, dst, local_sem.at[i])
        loads[name].start()
    barrier = pltpu.get_barrier_semaphore()
    peers = [partner] + chip_peers + y_peers
    for peer in peers:
        pl.semaphore_signal(barrier, inc=1, device_id=peer, device_id_type=MESH)

    sent = []
    used = [0]

    def fresh(n=1):
        used[0] += n
        return used[0] - n

    def start(src, dst, device, send_at, recv_at):
        pltpu.make_async_remote_copy(
            src_ref=src, dst_ref=dst, send_sem=send_sem.at[send_at],
            recv_sem=recv_sem.at[recv_at], device_id=device, device_id_type=MESH,
        ).start()

    def send(copies, span):
        mine = fresh()
        for src, dst, device in copies:
            start(src, dst, device, mine, mine)
        sent.append((mine, span))
        return mine, span

    def arrived(handle):
        mine, span = handle
        pltpu.make_async_copy(span, span, recv_sem.at[mine]).wait()

    def first(reverse):
        return (core == 1) if reverse else (core == 0)

    def decay_row(ref, i):
        return jnp.exp(ref[pl.ds(HALF * core + i, 1), :])

    def part(i):
        return slice(i * per_head, (i + 1) * per_head)

    parity = z % 2
    my_shard = parity * per_head + chip_at // 2
    pairs = nz // 2

    def stage_pair(own, par, i):
        here = pl.ds(i * per_head, per_head)
        return send([(own.at[1 - core, here], par.at[here], partner)], par.at[here])

    def stage_chip(own, par, chip, zin, i, sems, reverse):
        one = jnp.ones((1, DH), F32)
        w_own = jnp.where(first(reverse), decay_row(g_par, i), one)
        w_par = jnp.where(first(reverse), one, decay_row(g_own, i))
        chip[part(i)] = w_own * own[core, part(i)] + w_par * par[part(i)]

        def post(xx, zz):
            shard = i * per_head + (xx * nz + zz) // 2
            start(chip.at[shard], zin.at[chip_at], at(xx, zz, core), sems, sems)

        for dx in outward(nx):
            for p in outward(pairs):
                if p or dx:
                    post(shifted(x, dx, nx), 2 * shifted(z // 2, p, pairs) + i)

        @pl.when(parity != i)
        def _():
            post(x, 2 * (z // 2) + i)

        @pl.when(parity == i)
        def _():
            zin[chip_at] = chip[my_shard]

    def stage_fold(zin, pre, back, sems, reverse):
        all_others = zin.at[pl.ds(0, chips - 1)]
        arrived((sems, all_others))
        sent.append((sems, all_others))
        total = jnp.zeros((rows, DH), F32)
        for j in reversed(range(chips)) if reverse else range(chips):
            pre[j] = total
            total = decay[j, 0:1, :] * total + zin[j]
        mine = fresh(2)
        for (xx, zz), device in zip(others, chip_peers):
            start(pre.at[xx * nz + zz], back.at[my_shard], device, mine, mine + parity)
        sent.append((mine, all_others))
        back[my_shard] = pre[chip_at]
        return mine

    def stage_split(own, par, back, ent, pair, i, sems, reverse):
        @pl.when(parity != i)
        def _():
            arrived((sems + i, back.at[pl.ds(0, per_head)]))

        @pl.when(parity == i)
        def _():
            arrived((sems + i, back.at[pl.ds(0, per_head - 1)]))

        one, zero = jnp.ones((1, DH), F32), jnp.zeros((1, DH), F32)
        lead = first(reverse)
        here = pl.ds(i * per_head, per_head)
        w_par = jnp.where(lead, decay_row(g_own, i), one)
        s_par = jnp.where(lead, one, zero)
        pair[part(i)] = w_par * back[part(i)] + s_par * own[core, part(i)]
        handle = send([(pair.at[here], ent.at[core, here], partner)], pair.at[here])
        w_own = jnp.where(lead, one, decay_row(g_par, i))
        s_own = jnp.where(lead, zero, one)
        ent[core, part(i)] = w_own * back[part(i)] + s_own * par[part(i)]
        return handle

    def state_b(ent, half, i):
        return ent[half, part(i)].reshape(DH, DH).astype(BF16)

    loads["ld"].wait()
    cumul = lane_cumsum(jnp.concatenate([ld[...], ld[...]], axis=0))
    total = cumul[:, BLOCK - 1 :]
    g_own[...] = jnp.broadcast_to(total, (8, DH))
    ea, tail = jnp.exp(cumul), jnp.exp(total - cumul)
    row_form[0], row_form[1], row_form[2] = cumul, ea, tail
    loads["k"].wait()
    loads["v"].wait()
    def block_state(half, i):
        h = HALF * half + i
        weighted = (k[:, lanes(h)].T.astype(F32) * row_form[2, pl.ds(h, 1), :]).astype(BF16)
        f_own[half, part(i)] = nn(weighted, v[:, lanes(h)]).reshape(per_head, rows, DH)

    f_copies = []
    for i in range(HALF):
        block_state(1 - core, i)
        if i == 0:
            pl.semaphore_wait(barrier, len(peers))
            g_copies = send([(g_own, g_par, partner)], g_par)
        f_copies.append(stage_pair(f_own, f_par, i))
    for i in range(HALF):
        block_state(core, i)

    def spread():
        for kind in range(3):
            for h in range(HEADS):
                j = 8 * kind + h
                columns[kind, h] = jnp.broadcast_to(col_form[:, j : j + 1], (BLOCK, DH))

    def prepare(h):
        ea_here = columns[1, h]
        tail_here = columns[2, h]
        q_here = q[:, lanes(h)]
        wq[h] = (q_here.astype(F32) * ea_here).astype(BF16)
        wk[:, lanes(h)] = (k[:, lanes(h)].astype(F32) * tail_here).astype(BF16)
        wv[:, lanes(h)] = (v[:, lanes(h)].astype(F32) * tail_here).astype(BF16)
        turned_q = q_here.T
        qt[h] = turned_q
        wqt[h] = (turned_q.astype(F32) * row_form[1, pl.ds(h, 1), :]).astype(BF16)

    def intra(h):
        a_here = row_form[0, pl.ds(h, 1), :]
        a_col = columns[0, h]
        for t in range(0, BLOCK, TILE):
            seen = t + TILE
            here = slice(t, seen)
            scores = nt(q[here, lanes(h)], k[:seen, lanes(h)])
            col = jnp.concatenate([a_col[here]] * (seen // DH), axis=1)
            diff = col - a_here[:, :seen]
            keep = lax.broadcasted_iota(jnp.int32, diff.shape, 0) + t >= (
                lax.broadcasted_iota(jnp.int32, diff.shape, 1)
            )
            weight = jnp.where(keep, jnp.exp(jnp.where(keep, diff, 0.0)), 0.0)
            mask[h, here, :seen] = weight
            weights = (scores * weight).astype(BF16)
            fw[h, here, :seen] = weights
            att[here, lanes(h)] = nn(weights, v[:seen, lanes(h)])

    def gates(h):
        sig = jax.nn.sigmoid(gate[:, lanes(h)].astype(F32))
        normed = gout[:, lanes(h)].astype(F32) * sig * gain[:, lanes(h)]
        gn[:, lanes(h)] = normed
        gg[:, lanes(h)] = normed * (1.0 - sig)

    col_form[...] = turned(jnp.concatenate([cumul, ea, tail], axis=0))
    arrived(g_copies)
    g_all[chip_at] = g_own[...] + g_par[...]
    g_copies = send(
        [(g_all.at[chip_at], g_all.at[chip_at], peer) for peer in z_peers],
        g_all.at[pl.ds(0, nz - 1)],
    )
    spread()
    f_sems = fresh()
    for i in range(HALF):
        arrived(f_copies[i])
        stage_chip(f_own, f_par, f_chip, f_zin, i, f_sems, False)
    arrived(g_copies)
    row_at = pl.ds(x * nz, nz)
    g_copies = send(
        [(g_all.at[row_at], g_all.at[row_at], peer) for peer in x_peers],
        g_all.at[pl.ds(0, nz * (nx - 1))],
    )
    for name in ("q", "gate", "gout", "gain"):
        loads[name].wait()
    for i in range(HALF):
        h = HALF * (1 - core) + i
        prepare(h)
        intra(h)
        gates(h)
        x_out[0, i] = wq[h].astype(F32)
        x_out[1, i] = att[:, lanes(h)]
        x_out[2, i] = gn[:, lanes(h)]
    x_copies = send([(x_out, x_in, partner)], x_in)
    arrived(g_copies)
    for j in range(chips):
        decay[j] = jnp.broadcast_to(
            jnp.exp(g_all[j, pl.ds(HALF * core + parity, 1), :]), (8, DH)
        )
    f_sems = stage_fold(f_zin, f_pre, f_back, f_sems, False)
    for i in range(HALF):
        h = HALF * core + i
        prepare(h)
        intra(h)
        gates(h)
    arrived(x_copies)
    for i in range(HALF):
        wqt_par[i] = x_in[0, i].T.astype(BF16)

    def attend(h, entering):
        full = att[:, lanes(h)] + nn(wq[h], entering)
        att[:, lanes(h)] = full
        return full

    none = jnp.zeros((BLOCK, DH), F32)
    squares, inner, squares_par, inner_par = none, none, none, none
    f_copies = []
    for i in range(HALF):
        f_copies.append(
            stage_split(f_own, f_par, f_back, f_ent, f_pair, i, f_sems, False)
        )
        h = HALF * core + i
        full = attend(h, state_b(f_ent, core, i))
        squares = squares + full * full
        inner = inner + full * gn[:, lanes(h)]
        entering_par = f_pair[part(i)].reshape(DH, DH).astype(BF16)
        full = x_in[1, i] + nn(x_in[0, i].astype(BF16), entering_par)
        att_par[i] = full
        squares_par = squares_par + full * full
        inner_par = inner_par + full * x_in[2, i]

    ones = jnp.ones((8, DH), BF16)

    def row_sums(value):
        high = value.astype(BF16)
        low = (value - high.astype(F32)).astype(BF16)
        return nt(ones, high) + nt(ones, low)

    parts = BLOCK // DH

    def tile(*values):
        sums = [row_sums(value) for value in values]
        return jnp.concatenate(
            [s[0:1, i * DH : (i + 1) * DH] for s in sums for i in range(parts)], axis=0
        )

    y_out[core] = tile(squares, inner)
    y_out[1 - core] = tile(squares_par, inner_par)
    slot = 2 * head + core
    copies = send(
        [(y_out, y_in.at[slot], peer) for peer in y_peers + [partner]],
        y_in.at[pl.ds(0, 2 * nh - 1)],
    )
    y_in[slot] = y_out[...]
    arrived(copies)
    features = HEADS * DH * nh

    def row_scales(block):
        summed = y_in[0, block]
        for i in range(1, 2 * nh):
            summed = summed + y_in[i, block]
        rms = lax.rsqrt(summed[:parts] / features + 1e-05)
        return [rms, rms * rms * rms * summed[parts:] / features]

    scales = turned(jnp.concatenate(row_scales(core) + row_scales(1 - core), axis=0))

    def scale_column(first_lane):
        return jnp.concatenate(
            [
                jnp.broadcast_to(scales[:, i : i + 1], (DH, DH))
                for i in range(first_lane, first_lane + parts)
            ],
            axis=0,
        )

    rms_col, coef_col = scale_column(0), scale_column(parts)
    rms_par, coef_par = scale_column(2 * parts), scale_column(3 * parts)

    def gradient(h):
        grad = (rms_col * gn[:, lanes(h)] - att[:, lanes(h)] * coef_col).astype(BF16)
        gb[:, lanes(h)] = grad
        return grad

    r_sems = fresh()
    for i in range(HALF):
        h = HALF * core + i
        r_own[core, part(i)] = nn(wqt[h], gradient(h)).reshape(per_head, rows, DH)
        grad = (rms_par * x_in[2, i] - att_par[i] * coef_par).astype(BF16)
        r_par[part(i)] = nn(wqt_par[i], grad).reshape(per_head, rows, DH)
        stage_chip(r_own, r_par, r_chip, r_zin, i, r_sems, True)
    for i in range(HALF):
        h = HALF * (1 - core) + i
        arrived(f_copies[i])
        attend(h, state_b(f_ent, 1 - core, i))
        gradient(h)

    def back(h):
        grad = gb[:, lanes(h)]
        entering = state_b(f_ent, h // HALF, h % HALF)
        upper = []
        for t in range(0, BLOCK, TILE):
            seen = t + TILE
            here = slice(t, seen)
            weights = (nt(grad[here], v[:seen, lanes(h)]) * mask[h, here, :seen]).astype(BF16)
            upper.append(weights)
            dq[here, lanes(h)] = (
                nn(weights, k[:seen, lanes(h)]) + columns[1, h, here, :] * nt(grad[here], entering)
            ).astype(BF16)
        gt = grad.T
        for s in range(0, BLOCK, TILE):
            here = slice(s, s + TILE)
            key = value = None
            for t in range(s, BLOCK, TILE):
                there = slice(t, t + TILE)
                one_key = nn(qt[h, :, there], upper[t // TILE][:, here])
                one_value = nn(gt[:, there], fw[h, there, here])
                key = one_key if key is None else key + one_key
                value = one_value if value is None else value + one_value
            dki[here, lanes(h)] = key.T
            dvi[here, lanes(h)] = value.T

    for h in range(HEADS):
        dg[:, lanes(h)] = (gg[:, lanes(h)] * att[:, lanes(h)] * rms_col).astype(BF16)
    back(0)
    back(1)
    r_sems = stage_fold(r_zin, r_pre, r_back, r_sems, True)
    back(2)
    back(3)
    r_copies = [
        stage_split(r_own, r_par, r_back, r_ent, r_pair, i, r_sems, True)
        for i in range(HALF)
    ]
    for i in range(HALF):
        arrived(r_copies[i])
    for mine, span in sent:
        pltpu.make_async_copy(span, span, send_sem.at[mine]).wait()


def finish(
    dq_in, dg_in, dki, dvi, wk, wv, ent, dq_hbm, dk_hbm, dv_hbm, dg_hbm, dk, dv, sem
):
    copies = [
        pltpu.make_async_copy(dq_in, dq_hbm, sem.at[0]),
        pltpu.make_async_copy(dg_in, dg_hbm, sem.at[1]),
    ]
    for copy in copies:
        copy.start()
    for h in range(HEADS):
        leaving = ent[h].astype(BF16)
        dk[:, lanes(h)] = (dki[:, lanes(h)] + nt(wv[:, lanes(h)], leaving)).astype(BF16)
        dv[:, lanes(h)] = (dvi[:, lanes(h)] + nn(wk[:, lanes(h)], leaving)).astype(BF16)
        for i, (src, dst) in enumerate(((dk, dk_hbm), (dv, dv_hbm))):
            copy = pltpu.make_async_copy(
                src.at[:, lanes(h)], dst.at[:, lanes(h)], sem.at[2 + 2 * h + i]
            )
            copy.start()
            copies.append(copy)
    for copy in copies:
        copy.wait()


def build(nx, nz, nh):
    chips = nx * nz
    rows = HALF * DH // chips
    wide = (BLOCK, HEADS * DH)
    per_head = (HEADS, BLOCK, DH)

    def vmem(shape, dtype=F32):
        return pltpu.VMEM(shape, dtype)

    shards, halves = vmem((chips, rows, DH)), vmem((HALF, chips, rows, DH))
    scratch = (
        [vmem(wide, BF16)] * 5
        + [vmem((HEADS, BLOCK)), vmem((1, HEADS * DH))]
        + [vmem((3, 8, BLOCK)), vmem((BLOCK, DH)), vmem((3,) + per_head)]
        + [vmem((HEADS, DH, BLOCK), BF16)] * 2
        + [vmem(per_head, BF16)]
        + [vmem((HEADS, BLOCK, BLOCK)), vmem((HEADS, BLOCK, BLOCK), BF16)]
        + [vmem(wide)] * 3
        + [vmem(wide, BF16)]
        + [vmem((8, DH))] * 2
        + [vmem((chips, 8, DH))] * 2
        + [vmem((3, HALF, BLOCK, DH))] * 2
        + [vmem((HALF, BLOCK, DH)), vmem((HALF, DH, BLOCK), BF16)]
        + [halves, shards, shards, shards, shards, halves, shards, shards]
        + [halves, shards, shards, shards, shards, shards, shards]
        + [vmem((2, 8, DH)), vmem((2 * nh, 2, 8, DH))]
        + [pltpu.SemaphoreType.DMA((7,))]
        + [pltpu.SemaphoreType.DMA((17,))] * 2
    )
    any_space = pl.BlockSpec(memory_space=pl.ANY)
    in_vmem = pl.BlockSpec(memory_space=pltpu.VMEM)

    def local(q, k, v, gate, gout, log_decay, gain):
        made = pl.pallas_call(
            functools.partial(kernel, nx, nz, nh),
            out_shape=[kept(wide, BF16)] * 2
            + [kept(wide, F32)] * 2
            + [kept(wide, BF16)] * 2
            + [kept((HALF, chips, rows, DH), F32)],
            in_specs=[any_space] * 7,
            out_specs=[in_vmem] * 7,
            scratch_shapes=scratch,
            compiler_params=pltpu.CompilerParams(
                collective_id=0, has_side_effects=True, vmem_limit_bytes=36 * 2**20
            ),
        )(*placed(
            (q, k, v, gate, gout, log_decay.T, gain.reshape(1, HEADS * DH)), pltpu.HBM
        ))
        made = list(made)
        made[-1] = made[-1].reshape(HEADS, DH, DH)
        return tuple(
            pl.pallas_call(
                finish,
                out_shape=[jax.ShapeDtypeStruct(wide, BF16)] * 4,
                in_specs=[in_vmem] * 7,
                out_specs=[any_space] * 4,
                scratch_shapes=[vmem(wide, BF16)] * 2 + [pltpu.SemaphoreType.DMA((10,))],
                compiler_params=pltpu.CompilerParams(vmem_limit_bytes=8 * 2**20),
            )(*placed(made, pltpu.VMEM))
        )

    return local


def solution(mesh):
    nx, nz = NX, NZ
    if mesh.shape["ctx"] != 2 * nx * nz:
        nx = nz = 2
    part = P("ctx", "head")
    return jax.shard_map(
        build(nx, nz, mesh.shape["head"]),
        mesh=mesh,
        in_specs=(part,) * 6 + (P("head"),),
        out_specs=(part,) * 4,
        check_vma=False,
    )
```

```python
import functools

import jax
import jax.numpy as jnp
from jax import lax
from jax.experimental import pallas as pl
from jax.experimental.pallas import tpu as pltpu
from jax.sharding import PartitionSpec as P

BLOCK = 512
DH = 128
HEADS = 4
HALF = HEADS // 2
TILE = 256
NX = 4
NZ = 8
F32 = jnp.float32
BF16 = jnp.bfloat16
MESH = pl.DeviceIdType.MESH


def nn(a, b):
    return jnp.dot(a, b, preferred_element_type=F32)


def nt(a, b):
    return lax.dot_general(a, b, (((1,), (1,)), ((), ())), preferred_element_type=F32)


def lane_cumsum(x):
    place = lax.broadcasted_iota(jnp.int32, x.shape, 1)
    step = 1
    while step < x.shape[1]:
        x = x + jnp.where(place >= step, pltpu.roll(x, step, 1), 0.0)
        step *= 2
    return x


def turned(rows):
    pad = jnp.zeros((DH - rows.shape[0], rows.shape[1]), F32)
    return jnp.concatenate([rows, pad], axis=0).T


def kept(shape, dtype):
    return pltpu.VMEM(shape, dtype)


def placed(values, space):
    return [pltpu.with_memory_space_constraint(value, space) for value in values]


def lanes(h):
    return pl.ds(h * DH if isinstance(h, int) else pl.multiple_of(h * DH, DH), DH)


def kernel(
    nx, nz, nh,
    q_hbm, k_hbm, v_hbm, gate_hbm, gout_hbm, ld_hbm, gain_hbm,
    dq, dg, dk, dv, dki, dvi, wk, wv, r_ent,
    q, k, v, gate, gout, ld, gain,
    row_form, col_form, columns,
    qt, wqt, wq, mask, fw, att, gn, gg, gb,
    g_own, g_par, g_all, decay, x_out, x_in, att_par, wq_par, wqt_par,
    f_own, f_par, f_chip, f_zin, f_back, f_ent, f_pair, f_pre,
    r_own, r_par, r_chip, r_zin, r_back, r_pair, r_pre,
    y_out, y_in,
    local_sem, send_sem, recv_sem,
):
    me, head = lax.axis_index("ctx"), lax.axis_index("head")
    core, chip_at = me % 2, me // 2
    z, x = chip_at % nz, chip_at // nz
    chips = nx * nz
    rows = HALF * DH // chips
    per_head = chips // HALF

    def at(xx, zz, cc):
        return ((xx * nz + zz) * 2 + cc, head)

    partner = at(x, z, 1 - core)
    sign = 1 - 2 * core

    def shifted(place, d, n):
        return (place + n + sign * d) % n

    def outward(n):
        return sorted(range(n), key=lambda d: -min(d, n - d))

    steps = [(dx, dz) for dx in outward(nx) for dz in outward(nz) if (dx, dz) != (0, 0)]
    others = [(shifted(x, dx, nx), shifted(z, dz, nz)) for dx, dz in steps]
    z_peers = [at(x, (z + d) % nz, core) for d in range(1, nz)]
    x_peers = [at((x + d) % nx, z, core) for d in range(1, nx)]
    chip_peers = [at(xx, zz, core) for xx, zz in others]
    y_peers = [
        (at(x, z, c)[0], shifted(head, d, nh))
        for d in outward(nh)
        for c in (core, 1 - core)
        if d
    ]

    loads = {}
    for i, (name, src, dst) in enumerate((
        ("ld", ld_hbm, ld), ("k", k_hbm, k), ("v", v_hbm, v), ("q", q_hbm, q),
        ("gate", gate_hbm, gate), ("gout", gout_hbm, gout), ("gain", gain_hbm, gain),
    )):
        loads[name] = pltpu.make_async_copy(src, dst, local_sem.at[i])
        loads[name].start()
    barrier = pltpu.get_barrier_semaphore()
    peers = [partner] + chip_peers + y_peers
    for peer in peers:
        pl.semaphore_signal(barrier, inc=1, device_id=peer, device_id_type=MESH)

    sent = []
    used = [0]

    def fresh(n=1):
        used[0] += n
        return used[0] - n

    def start(src, dst, device, send_at, recv_at):
        pltpu.make_async_remote_copy(
            src_ref=src, dst_ref=dst, send_sem=send_sem.at[send_at],
            recv_sem=recv_sem.at[recv_at], device_id=device, device_id_type=MESH,
        ).start()

    def send(copies, span):
        mine = fresh()
        for src, dst, device in copies:
            start(src, dst, device, mine, mine)
        sent.append((mine, span))
        return mine, span

    def arrived(handle):
        mine, span = handle
        pltpu.make_async_copy(span, span, recv_sem.at[mine]).wait()

    def first(reverse):
        return (core == 1) if reverse else (core == 0)

    def decay_row(ref, i):
        return jnp.exp(ref[pl.ds(HALF * core + i, 1), :])

    def part(i):
        return slice(i * per_head, (i + 1) * per_head)

    parity = z % 2
    my_shard = parity * per_head + chip_at // 2
    pairs = nz // 2

    def stage_pair(own, par, i):
        here = pl.ds(i * per_head, per_head)
        return send([(own.at[1 - core, here], par.at[here], partner)], par.at[here])

    def stage_chip(own, par, chip, zin, i, sems, reverse):
        one = jnp.ones((1, DH), F32)
        w_own = jnp.where(first(reverse), decay_row(g_par, i), one)
        w_par = jnp.where(first(reverse), one, decay_row(g_own, i))
        chip[part(i)] = w_own * own[core, part(i)] + w_par * par[part(i)]

        def post(xx, zz):
            shard = i * per_head + (xx * nz + zz) // 2
            start(chip.at[shard], zin.at[chip_at], at(xx, zz, core), sems, sems)

        for dx in outward(nx):
            for p in outward(pairs):
                if p or dx:
                    post(shifted(x, dx, nx), 2 * shifted(z // 2, p, pairs) + i)

        @pl.when(parity != i)
        def _():
            post(x, 2 * (z // 2) + i)

        @pl.when(parity == i)
        def _():
            zin[chip_at] = chip[my_shard]

    def stage_fold(zin, pre, back, sems, reverse):
        all_others = zin.at[pl.ds(0, chips - 1)]
        arrived((sems, all_others))
        sent.append((sems, all_others))
        total = jnp.zeros((rows, DH), F32)
        for j in reversed(range(chips)) if reverse else range(chips):
            pre[j] = total
            total = decay[j, 0:1, :] * total + zin[j]
        mine = fresh(2)
        for (xx, zz), device in zip(others, chip_peers):
            start(pre.at[xx * nz + zz], back.at[my_shard], device, mine, mine + parity)
        sent.append((mine, all_others))
        back[my_shard] = pre[chip_at]
        return mine

    def stage_split(own, par, back, ent, pair, i, sems, reverse):
        @pl.when(parity != i)
        def _():
            arrived((sems + i, back.at[pl.ds(0, per_head)]))

        @pl.when(parity == i)
        def _():
            arrived((sems + i, back.at[pl.ds(0, per_head - 1)]))

        one, zero = jnp.ones((1, DH), F32), jnp.zeros((1, DH), F32)
        lead = first(reverse)
        here = pl.ds(i * per_head, per_head)
        w_par = jnp.where(lead, decay_row(g_own, i), one)
        s_par = jnp.where(lead, one, zero)
        pair[part(i)] = w_par * back[part(i)] + s_par * own[core, part(i)]
        handle = send([(pair.at[here], ent.at[core, here], partner)], pair.at[here])
        w_own = jnp.where(lead, one, decay_row(g_par, i))
        s_own = jnp.where(lead, zero, one)
        ent[core, part(i)] = w_own * back[part(i)] + s_own * par[part(i)]
        return handle

    def state_b(ent, half, i):
        return ent[half, part(i)].reshape(DH, DH).astype(BF16)

    loads["ld"].wait()
    cumul = lane_cumsum(jnp.concatenate([ld[...], ld[...]], axis=0))
    total = cumul[:, BLOCK - 1 :]
    g_own[...] = jnp.broadcast_to(total, (8, DH))
    ea, tail = jnp.exp(cumul), jnp.exp(total - cumul)
    row_form[0], row_form[1], row_form[2] = cumul, ea, tail
    loads["k"].wait()
    loads["v"].wait()
    def block_state(half, i):
        h = HALF * half + i
        weighted = (k[:, lanes(h)].T.astype(F32) * row_form[2, pl.ds(h, 1), :]).astype(BF16)
        f_own[half, part(i)] = nn(weighted, v[:, lanes(h)]).reshape(per_head, rows, DH)

    f_copies = []
    for i in range(HALF):
        block_state(1 - core, i)
        if i == 0:
            pl.semaphore_wait(barrier, len(peers))
            g_copies = send([(g_own, g_par, partner)], g_par)
        f_copies.append(stage_pair(f_own, f_par, i))
    for i in range(HALF):
        block_state(core, i)

    def spread():
        for kind in range(3):
            for h in range(HEADS):
                j = 8 * kind + h
                columns[kind, h] = jnp.broadcast_to(col_form[:, j : j + 1], (BLOCK, DH))

    def prepare(h):
        ea_here = columns[1, h]
        tail_here = columns[2, h]
        q_here = q[:, lanes(h)]
        wq[h] = (q_here.astype(F32) * ea_here).astype(BF16)
        wk[:, lanes(h)] = (k[:, lanes(h)].astype(F32) * tail_here).astype(BF16)
        wv[:, lanes(h)] = (v[:, lanes(h)].astype(F32) * tail_here).astype(BF16)
        turned_q = q_here.T
        qt[h] = turned_q
        wqt[h] = (turned_q.astype(F32) * row_form[1, pl.ds(h, 1), :]).astype(BF16)

    def intra(h):
        a_here = row_form[0, pl.ds(h, 1), :]
        a_col = columns[0, h]
        for t in range(0, BLOCK, TILE):
            seen = t + TILE
            here = slice(t, seen)
            scores = nt(q[here, lanes(h)], k[:seen, lanes(h)])
            col = jnp.concatenate([a_col[here]] * (seen // DH), axis=1)
            diff = col - a_here[:, :seen]
            keep = lax.broadcasted_iota(jnp.int32, diff.shape, 0) + t >= (
                lax.broadcasted_iota(jnp.int32, diff.shape, 1)
            )
            weight = jnp.where(keep, jnp.exp(jnp.where(keep, diff, 0.0)), 0.0)
            mask[h, here, :seen] = weight
            weights = (scores * weight).astype(BF16)
            fw[h, here, :seen] = weights
            att[here, lanes(h)] = nn(weights, v[:seen, lanes(h)])

    def gates(h):
        sig = jax.nn.sigmoid(gate[:, lanes(h)].astype(F32))
        normed = gout[:, lanes(h)].astype(F32) * sig * gain[:, lanes(h)]
        gn[:, lanes(h)] = normed
        gg[:, lanes(h)] = normed * (1.0 - sig)

    col_form[...] = turned(jnp.concatenate([cumul, ea, tail], axis=0))
    arrived(g_copies)
    g_all[chip_at] = g_own[...] + g_par[...]
    g_copies = send(
        [(g_all.at[chip_at], g_all.at[chip_at], peer) for peer in z_peers],
        g_all.at[pl.ds(0, nz - 1)],
    )
    spread()
    f_sems = fresh()
    for i in range(HALF):
        arrived(f_copies[i])
        stage_chip(f_own, f_par, f_chip, f_zin, i, f_sems, False)
    arrived(g_copies)
    row_at = pl.ds(x * nz, nz)
    g_copies = send(
        [(g_all.at[row_at], g_all.at[row_at], peer) for peer in x_peers],
        g_all.at[pl.ds(0, nz * (nx - 1))],
    )
    for name in ("q", "gate", "gout", "gain"):
        loads[name].wait()
    x_copies = []
    for i in range(HALF):
        h = HALF * (1 - core) + i
        prepare(h)
        intra(h)
        gates(h)
        x_out[i, 0] = wq[h].astype(F32)
        x_out[i, 1] = att[:, lanes(h)]
        x_out[i, 2] = gn[:, lanes(h)]
        x_copies.append(send([(x_out.at[i], x_in.at[i], partner)], x_in.at[i]))
    arrived(g_copies)
    for j in range(chips):
        decay[j] = jnp.broadcast_to(
            jnp.exp(g_all[j, pl.ds(HALF * core + parity, 1), :]), (8, DH)
        )
    f_sems = stage_fold(f_zin, f_pre, f_back, f_sems, False)
    for i in range(HALF):
        h = HALF * core + i
        prepare(h)
        intra(h)
        gates(h)
    for i in range(HALF):
        arrived(x_copies[i])
        wq_par[i] = x_in[i, 0].astype(BF16)
        wqt_par[i] = x_in[i, 0].T.astype(BF16)

    def attend(h, entering):
        full = att[:, lanes(h)] + nn(wq[h], entering)
        att[:, lanes(h)] = full
        return full

    none = jnp.zeros((BLOCK, DH), F32)
    squares, inner, squares_par, inner_par = none, none, none, none
    f_copies = []
    for i in range(HALF):
        f_copies.append(
            stage_split(f_own, f_par, f_back, f_ent, f_pair, i, f_sems, False)
        )
        h = HALF * core + i
        full = attend(h, state_b(f_ent, core, i))
        squares = squares + full * full
        inner = inner + full * gn[:, lanes(h)]
        entering_par = f_pair[part(i)].reshape(DH, DH).astype(BF16)
        full = x_in[i, 1] + nn(wq_par[i], entering_par)
        att_par[i] = full
        squares_par = squares_par + full * full
        inner_par = inner_par + full * x_in[i, 2]

    ones = jnp.ones((8, DH), BF16)

    def row_sums(value):
        return nt(ones, value.astype(BF16))

    parts = BLOCK // DH

    def tile(*values):
        sums = [row_sums(value) for value in values]
        return jnp.concatenate(
            [s[0:1, i * DH : (i + 1) * DH] for s in sums for i in range(parts)], axis=0
        )

    y_out[core] = tile(squares, inner)
    y_out[1 - core] = tile(squares_par, inner_par)
    slot = 2 * head + core
    copies = send(
        [(y_out, y_in.at[slot], peer) for peer in y_peers + [partner]],
        y_in.at[pl.ds(0, 2 * nh - 1)],
    )
    y_in[slot] = y_out[...]
    arrived(copies)
    features = HEADS * DH * nh

    def row_scales(block):
        summed = y_in[0, block]
        for i in range(1, 2 * nh):
            summed = summed + y_in[i, block]
        rms = lax.rsqrt(summed[:parts] / features + 1e-05)
        return [rms, rms * rms * rms * summed[parts:] / features]

    scales = turned(jnp.concatenate(row_scales(core) + row_scales(1 - core), axis=0))

    def scale_column(first_lane):
        return jnp.concatenate(
            [
                jnp.broadcast_to(scales[:, i : i + 1], (DH, DH))
                for i in range(first_lane, first_lane + parts)
            ],
            axis=0,
        )

    rms_col, coef_col = scale_column(0), scale_column(parts)
    rms_par, coef_par = scale_column(2 * parts), scale_column(3 * parts)

    def gradient(h):
        grad = (rms_col * gn[:, lanes(h)] - att[:, lanes(h)] * coef_col).astype(BF16)
        gb[:, lanes(h)] = grad
        return grad

    r_sems = fresh()
    for i in range(HALF):
        h = HALF * core + i
        r_own[core, part(i)] = nn(wqt[h], gradient(h)).reshape(per_head, rows, DH)
        grad = (rms_par * x_in[i, 2] - att_par[i] * coef_par).astype(BF16)
        r_par[part(i)] = nn(wqt_par[i], grad).reshape(per_head, rows, DH)
        stage_chip(r_own, r_par, r_chip, r_zin, i, r_sems, True)
    for i in range(HALF):
        h = HALF * (1 - core) + i
        arrived(f_copies[i])
        attend(h, state_b(f_ent, 1 - core, i))
        gradient(h)

    def back(h):
        grad = gb[:, lanes(h)]
        entering = state_b(f_ent, h // HALF, h % HALF)
        upper = []
        for t in range(0, BLOCK, TILE):
            seen = t + TILE
            here = slice(t, seen)
            weights = (nt(grad[here], v[:seen, lanes(h)]) * mask[h, here, :seen]).astype(BF16)
            upper.append(weights)
            dq[here, lanes(h)] = (
                nn(weights, k[:seen, lanes(h)]) + columns[1, h, here, :] * nt(grad[here], entering)
            ).astype(BF16)
        gt = grad.T
        for s in range(0, BLOCK, TILE):
            here = slice(s, s + TILE)
            key = value = None
            for t in range(s, BLOCK, TILE):
                there = slice(t, t + TILE)
                one_key = nn(qt[h, :, there], upper[t // TILE][:, here])
                one_value = nn(gt[:, there], fw[h, there, here])
                key = one_key if key is None else key + one_key
                value = one_value if value is None else value + one_value
            dki[here, lanes(h)] = key.T
            dvi[here, lanes(h)] = value.T

    for h in range(HEADS):
        dg[:, lanes(h)] = (gg[:, lanes(h)] * att[:, lanes(h)] * rms_col).astype(BF16)
    back(0)
    back(1)
    r_sems = stage_fold(r_zin, r_pre, r_back, r_sems, True)
    back(2)
    back(3)
    r_copies = [
        stage_split(r_own, r_par, r_back, r_ent, r_pair, i, r_sems, True)
        for i in range(HALF)
    ]
    for i in range(HALF):
        here = lanes(HALF * core + i)
        leaving = state_b(r_ent, core, i)
        dk[:, here] = (dki[:, here] + nt(wv[:, here], leaving)).astype(BF16)
        dv[:, here] = (dvi[:, here] + nn(wk[:, here], leaving)).astype(BF16)
    for i in range(HALF):
        arrived(r_copies[i])
    for mine, span in sent:
        pltpu.make_async_copy(span, span, send_sem.at[mine]).wait()


def finish(
    dq_in, dg_in, dk_in, dv_in, dki, dvi, wk, wv, ent,
    dq_hbm, dk_hbm, dv_hbm, dg_hbm, dk, dv, sem,
):
    core = lax.axis_index("ctx") % 2
    copies = []

    def store(src, dst):
        copy = pltpu.make_async_copy(src, dst, sem.at[len(copies)])
        copy.start()
        copies.append(copy)

    store(dq_in, dq_hbm)
    store(dg_in, dg_hbm)
    mine = pl.ds(pl.multiple_of(core * HALF * DH, DH), HALF * DH)
    store(dk_in.at[:, mine], dk_hbm.at[:, mine])
    store(dv_in.at[:, mine], dv_hbm.at[:, mine])
    for i in range(HALF):
        h = HALF * (1 - core) + i
        leaving = ent[h].astype(BF16)
        dk[i] = (dki[:, lanes(h)] + nt(wv[:, lanes(h)], leaving)).astype(BF16)
        store(dk.at[i], dk_hbm.at[:, lanes(h)])
        dv[i] = (dvi[:, lanes(h)] + nn(wk[:, lanes(h)], leaving)).astype(BF16)
        store(dv.at[i], dv_hbm.at[:, lanes(h)])
    for copy in copies:
        copy.wait()


def build(nx, nz, nh):
    chips = nx * nz
    rows = HALF * DH // chips
    wide = (BLOCK, HEADS * DH)
    per_head = (HEADS, BLOCK, DH)

    def vmem(shape, dtype=F32):
        return pltpu.VMEM(shape, dtype)

    shards, halves = vmem((chips, rows, DH)), vmem((HALF, chips, rows, DH))
    scratch = (
        [vmem(wide, BF16)] * 5
        + [vmem((HEADS, BLOCK)), vmem((1, HEADS * DH))]
        + [vmem((3, 8, BLOCK)), vmem((BLOCK, DH)), vmem((3,) + per_head)]
        + [vmem((HEADS, DH, BLOCK), BF16)] * 2
        + [vmem(per_head, BF16)]
        + [vmem((HEADS, BLOCK, BLOCK)), vmem((HEADS, BLOCK, BLOCK), BF16)]
        + [vmem(wide)] * 3
        + [vmem(wide, BF16)]
        + [vmem((8, DH))] * 2
        + [vmem((chips, 8, DH))] * 2
        + [vmem((HALF, 3, BLOCK, DH))] * 2
        + [vmem((HALF, BLOCK, DH)), vmem((HALF, BLOCK, DH), BF16)]
        + [vmem((HALF, DH, BLOCK), BF16)]
        + [halves, shards, shards, shards, shards, halves, shards, shards]
        + [halves, shards, shards, shards, shards, shards, shards]
        + [vmem((2, 8, DH)), vmem((2 * nh, 2, 8, DH))]
        + [pltpu.SemaphoreType.DMA((7,))]
        + [pltpu.SemaphoreType.DMA((18,))] * 2
    )
    any_space = pl.BlockSpec(memory_space=pl.ANY)
    in_vmem = pl.BlockSpec(memory_space=pltpu.VMEM)

    def local(q, k, v, gate, gout, log_decay, gain):
        made = pl.pallas_call(
            functools.partial(kernel, nx, nz, nh),
            out_shape=[kept(wide, BF16)] * 4
            + [kept(wide, F32)] * 2
            + [kept(wide, BF16)] * 2
            + [kept((HALF, chips, rows, DH), F32)],
            in_specs=[any_space] * 7,
            out_specs=[in_vmem] * 9,
            scratch_shapes=scratch,
            compiler_params=pltpu.CompilerParams(
                collective_id=0, has_side_effects=True, vmem_limit_bytes=36 * 2**20
            ),
        )(*placed(
            (q, k, v, gate, gout, log_decay.T, gain.reshape(1, HEADS * DH)), pltpu.HBM
        ))
        made = list(made)
        made[-1] = made[-1].reshape(HEADS, DH, DH)
        return tuple(
            pl.pallas_call(
                finish,
                out_shape=[jax.ShapeDtypeStruct(wide, BF16)] * 4,
                in_specs=[in_vmem] * 9,
                out_specs=[any_space] * 4,
                scratch_shapes=[vmem((HALF, BLOCK, DH), BF16)] * 2
                + [pltpu.SemaphoreType.DMA((8,))],
                compiler_params=pltpu.CompilerParams(vmem_limit_bytes=8 * 2**20),
            )(*placed(made, pltpu.VMEM))
        )

    return local


def solution(mesh):
    nx, nz = NX, NZ
    if mesh.shape["ctx"] != 2 * nx * nz:
        nx = nz = 2
    part = P("ctx", "head")
    return jax.shard_map(
        build(nx, nz, mesh.shape["head"]),
        mesh=mesh,
        in_specs=(part,) * 6 + (P("head"),),
        out_specs=(part,) * 4,
        check_vma=False,
    )
```

```python
import functools

import jax
import jax.numpy as jnp
from jax import lax
from jax.experimental import pallas as pl
from jax.experimental.pallas import tpu as pltpu
from jax.sharding import PartitionSpec as P

BLOCK = 512
DH = 128
HEADS = 4
HALF = HEADS // 2
TILE = 256
NX = 4
NZ = 8
F32 = jnp.float32
BF16 = jnp.bfloat16
MESH = pl.DeviceIdType.MESH


def nn(a, b):
    return jnp.dot(a, b, preferred_element_type=F32)


def nt(a, b):
    return lax.dot_general(a, b, (((1,), (1,)), ((), ())), preferred_element_type=F32)


def lane_cumsum(x):
    place = lax.broadcasted_iota(jnp.int32, x.shape, 1)
    step = 1
    while step < x.shape[1]:
        x = x + jnp.where(place >= step, pltpu.roll(x, step, 1), 0.0)
        step *= 2
    return x


def turned(rows):
    pad = jnp.zeros((DH - rows.shape[0], rows.shape[1]), F32)
    return jnp.concatenate([rows, pad], axis=0).T


def kept(shape, dtype):
    return pltpu.VMEM(shape, dtype)


def placed(values, space):
    return [pltpu.with_memory_space_constraint(value, space) for value in values]


def lanes(h):
    return pl.ds(h * DH if isinstance(h, int) else pl.multiple_of(h * DH, DH), DH)


def kernel(
    nx, nz, nh,
    q_hbm, k_hbm, v_hbm, gate_hbm, gout_hbm, ld_hbm, gain_hbm,
    dq, dg, dk, dv, dki, dvi, wk, wv, r_ent,
    q, k, v, gate, gout, ld, gain,
    row_form, col_form, columns,
    qt, wqt, wq, mask, fw, att, gn, gg, gb,
    g_own, g_par, g_all, decay, x_out, x_in, att_par, wq_par, wqt_par,
    f_own, f_par, f_chip, f_zin, f_back, f_ent, f_pair, f_pre,
    r_own, r_par, r_chip, r_zin, r_back, r_pair, r_pre,
    y_out, y_in,
    local_sem, send_sem, recv_sem,
):
    me, head = lax.axis_index("ctx"), lax.axis_index("head")
    core, chip_at = me % 2, me // 2
    z, x = chip_at % nz, chip_at // nz
    chips = nx * nz
    rows = HALF * DH // chips
    per_head = chips // HALF

    def at(xx, zz, cc):
        return ((xx * nz + zz) * 2 + cc, head)

    partner = at(x, z, 1 - core)
    sign = 1 - 2 * core

    def shifted(place, d, n):
        return (place + n + sign * d) % n

    def outward(n):
        return sorted(range(n), key=lambda d: -min(d, n - d))

    steps = [(dx, dz) for dx in outward(nx) for dz in outward(nz) if (dx, dz) != (0, 0)]
    others = [(shifted(x, dx, nx), shifted(z, dz, nz)) for dx, dz in steps]
    z_peers = [at(x, (z + d) % nz, core) for d in range(1, nz)]
    x_peers = [at((x + d) % nx, z, core) for d in range(1, nx)]
    chip_peers = [at(xx, zz, core) for xx, zz in others]
    y_peers = [
        (at(x, z, c)[0], shifted(head, d, nh))
        for d in outward(nh)
        for c in (core, 1 - core)
        if d
    ]

    loads = {}
    for i, (name, src, dst) in enumerate((
        ("ld", ld_hbm, ld), ("k", k_hbm, k), ("v", v_hbm, v), ("q", q_hbm, q),
        ("gate", gate_hbm, gate), ("gout", gout_hbm, gout), ("gain", gain_hbm, gain),
    )):
        loads[name] = pltpu.make_async_copy(src, dst, local_sem.at[i])
        loads[name].start()
    barrier = pltpu.get_barrier_semaphore()
    peers = [partner] + chip_peers + y_peers
    for peer in peers:
        pl.semaphore_signal(barrier, inc=1, device_id=peer, device_id_type=MESH)

    sent = []
    used = [0]

    def fresh(n=1):
        used[0] += n
        return used[0] - n

    def start(src, dst, device, send_at, recv_at):
        pltpu.make_async_remote_copy(
            src_ref=src, dst_ref=dst, send_sem=send_sem.at[send_at],
            recv_sem=recv_sem.at[recv_at], device_id=device, device_id_type=MESH,
        ).start()

    def send(copies, span):
        mine = fresh()
        for src, dst, device in copies:
            start(src, dst, device, mine, mine)
        sent.append((mine, span))
        return mine, span

    def arrived(handle):
        mine, span = handle
        pltpu.make_async_copy(span, span, recv_sem.at[mine]).wait()

    def first(reverse):
        return (core == 1) if reverse else (core == 0)

    def decay_row(ref, i):
        return jnp.exp(ref[pl.ds(HALF * core + i, 1), :])

    def part(i):
        return slice(i * per_head, (i + 1) * per_head)

    parity = z % 2
    my_shard = parity * per_head + chip_at // 2
    pairs = nz // 2

    def stage_pair(own, par, i):
        here = pl.ds(i * per_head, per_head)
        return send([(own.at[1 - core, here], par.at[here], partner)], par.at[here])

    def stage_chip(own, par, chip, zin, i, sems, reverse):
        one = jnp.ones((1, DH), F32)
        w_own = jnp.where(first(reverse), decay_row(g_par, i), one)
        w_par = jnp.where(first(reverse), one, decay_row(g_own, i))
        chip[part(i)] = w_own * own[core, part(i)] + w_par * par[part(i)]

        def post(xx, zz):
            shard = i * per_head + (xx * nz + zz) // 2
            start(chip.at[shard], zin.at[chip_at], at(xx, zz, core), sems, sems)

        for dx in outward(nx):
            for p in outward(pairs):
                if p or dx:
                    post(shifted(x, dx, nx), 2 * shifted(z // 2, p, pairs) + i)

        @pl.when(parity != i)
        def _():
            post(x, 2 * (z // 2) + i)

        @pl.when(parity == i)
        def _():
            zin[chip_at] = chip[my_shard]

    def stage_fold(zin, pre, back, sems, reverse):
        all_others = zin.at[pl.ds(0, chips - 1)]
        arrived((sems, all_others))
        sent.append((sems, all_others))
        total = jnp.zeros((rows, DH), F32)
        for j in reversed(range(chips)) if reverse else range(chips):
            pre[j] = total
            total = decay[j, 0:1, :] * total + zin[j]
        mine = fresh(2)
        for (xx, zz), device in zip(others, chip_peers):
            start(pre.at[xx * nz + zz], back.at[my_shard], device, mine, mine + parity)
        sent.append((mine, all_others))
        back[my_shard] = pre[chip_at]
        return mine

    def stage_split(own, par, back, ent, pair, i, sems, reverse):
        @pl.when(parity != i)
        def _():
            arrived((sems + i, back.at[pl.ds(0, per_head)]))

        @pl.when(parity == i)
        def _():
            arrived((sems + i, back.at[pl.ds(0, per_head - 1)]))

        one, zero = jnp.ones((1, DH), F32), jnp.zeros((1, DH), F32)
        lead = first(reverse)
        here = pl.ds(i * per_head, per_head)
        w_par = jnp.where(lead, decay_row(g_own, i), one)
        s_par = jnp.where(lead, one, zero)
        pair[part(i)] = w_par * back[part(i)] + s_par * own[core, part(i)]
        handle = send([(pair.at[here], ent.at[core, here], partner)], pair.at[here])
        w_own = jnp.where(lead, one, decay_row(g_par, i))
        s_own = jnp.where(lead, zero, one)
        ent[core, part(i)] = w_own * back[part(i)] + s_own * par[part(i)]
        return handle

    def state_b(ent, half, i):
        return ent[half, part(i)].reshape(DH, DH).astype(BF16)

    loads["ld"].wait()
    cumul = lane_cumsum(jnp.concatenate([ld[...], ld[...]], axis=0))
    total = cumul[:, BLOCK - 1 :]
    g_own[...] = jnp.broadcast_to(total, (8, DH))
    ea, tail = jnp.exp(cumul), jnp.exp(total - cumul)
    row_form[0], row_form[1], row_form[2] = cumul, ea, tail
    loads["k"].wait()
    loads["v"].wait()
    def block_state(half, i):
        h = HALF * half + i
        weighted = (k[:, lanes(h)].T.astype(F32) * row_form[2, pl.ds(h, 1), :]).astype(BF16)
        f_own[half, part(i)] = nn(weighted, v[:, lanes(h)]).reshape(per_head, rows, DH)

    f_copies = []
    for i in range(HALF):
        block_state(1 - core, i)
        if i == 0:
            pl.semaphore_wait(barrier, len(peers))
            g_copies = send([(g_own, g_par, partner)], g_par)
        f_copies.append(stage_pair(f_own, f_par, i))
    for i in range(HALF):
        block_state(core, i)

    def spread():
        for kind in range(3):
            for h in range(HEADS):
                j = 8 * kind + h
                columns[kind, h] = jnp.broadcast_to(col_form[:, j : j + 1], (BLOCK, DH))

    def prepare(h):
        ea_here = columns[1, h]
        tail_here = columns[2, h]
        q_here = q[:, lanes(h)]
        wq[h] = (q_here.astype(F32) * ea_here).astype(BF16)
        wk[:, lanes(h)] = (k[:, lanes(h)].astype(F32) * tail_here).astype(BF16)
        wv[:, lanes(h)] = (v[:, lanes(h)].astype(F32) * tail_here).astype(BF16)
        turned_q = q_here.T
        qt[h] = turned_q
        wqt[h] = (turned_q.astype(F32) * row_form[1, pl.ds(h, 1), :]).astype(BF16)

    def intra(h):
        a_here = row_form[0, pl.ds(h, 1), :]
        a_col = columns[0, h]
        for t in range(0, BLOCK, TILE):
            seen = t + TILE
            here = slice(t, seen)
            scores = nt(q[here, lanes(h)], k[:seen, lanes(h)])
            col = jnp.concatenate([a_col[here]] * (seen // DH), axis=1)
            diff = col - a_here[:, :seen]
            keep = lax.broadcasted_iota(jnp.int32, diff.shape, 0) + t >= (
                lax.broadcasted_iota(jnp.int32, diff.shape, 1)
            )
            weight = jnp.where(keep, jnp.exp(jnp.where(keep, diff, 0.0)), 0.0)
            mask[h, here, :seen] = weight
            weights = (scores * weight).astype(BF16)
            fw[h, here, :seen] = weights
            att[here, lanes(h)] = nn(weights, v[:seen, lanes(h)])

    def gates(h):
        sig = jax.nn.sigmoid(gate[:, lanes(h)].astype(F32))
        normed = gout[:, lanes(h)].astype(F32) * sig * gain[:, lanes(h)]
        gn[:, lanes(h)] = normed
        gg[:, lanes(h)] = normed * (1.0 - sig)

    col_form[...] = turned(jnp.concatenate([cumul, ea, tail], axis=0))
    arrived(g_copies)
    g_all[chip_at] = g_own[...] + g_par[...]
    g_copies = send(
        [(g_all.at[chip_at], g_all.at[chip_at], peer) for peer in z_peers],
        g_all.at[pl.ds(0, nz - 1)],
    )
    spread()
    f_sems = fresh()
    for i in range(HALF):
        arrived(f_copies[i])
        stage_chip(f_own, f_par, f_chip, f_zin, i, f_sems, False)
    arrived(g_copies)
    row_at = pl.ds(x * nz, nz)
    g_copies = send(
        [(g_all.at[row_at], g_all.at[row_at], peer) for peer in x_peers],
        g_all.at[pl.ds(0, nz * (nx - 1))],
    )
    for name in ("q", "gate", "gout", "gain"):
        loads[name].wait()
    x_copies = []
    for i in range(HALF):
        h = HALF * (1 - core) + i
        prepare(h)
        intra(h)
        gates(h)
        x_out[i, 0] = wq[h].astype(F32)
        x_out[i, 1] = att[:, lanes(h)]
        x_out[i, 2] = gn[:, lanes(h)]
        x_copies.append(send([(x_out.at[i], x_in.at[i], partner)], x_in.at[i]))
    arrived(g_copies)
    for j in range(chips):
        decay[j] = jnp.broadcast_to(
            jnp.exp(g_all[j, pl.ds(HALF * core + parity, 1), :]), (8, DH)
        )
    f_sems = stage_fold(f_zin, f_pre, f_back, f_sems, False)
    for i in range(HALF):
        h = HALF * core + i
        prepare(h)
        intra(h)
        gates(h)
    for i in range(HALF):
        arrived(x_copies[i])
        wq_par[i] = x_in[i, 0].astype(BF16)
        wqt_par[i] = x_in[i, 0].T.astype(BF16)

    def attend(h, entering):
        full = att[:, lanes(h)] + nn(wq[h], entering)
        att[:, lanes(h)] = full
        return full

    none = jnp.zeros((BLOCK, DH), F32)
    squares, inner, squares_par, inner_par = none, none, none, none
    f_copies = []
    for i in range(HALF):
        f_copies.append(
            stage_split(f_own, f_par, f_back, f_ent, f_pair, i, f_sems, False)
        )
        h = HALF * core + i
        full = attend(h, state_b(f_ent, core, i))
        squares = squares + full * full
        inner = inner + full * gn[:, lanes(h)]
        entering_par = f_pair[part(i)].reshape(DH, DH).astype(BF16)
        full = x_in[i, 1] + nn(wq_par[i], entering_par)
        att_par[i] = full
        squares_par = squares_par + full * full
        inner_par = inner_par + full * x_in[i, 2]

    ones = jnp.ones((8, DH), BF16)

    def row_sums(value):
        return nt(ones, value.astype(BF16))

    parts = BLOCK // DH

    def tile(*values):
        sums = [row_sums(value) for value in values]
        return jnp.concatenate(
            [s[0:1, i * DH : (i + 1) * DH] for s in sums for i in range(parts)], axis=0
        )

    y_out[core] = tile(squares, inner)
    y_out[1 - core] = tile(squares_par, inner_par)
    slot = 2 * head + core
    copies = send(
        [(y_out, y_in.at[slot], peer) for peer in y_peers + [partner]],
        y_in.at[pl.ds(0, 2 * nh - 1)],
    )
    y_in[slot] = y_out[...]
    arrived(copies)
    features = HEADS * DH * nh

    def row_scales(block):
        summed = y_in[0, block]
        for i in range(1, 2 * nh):
            summed = summed + y_in[i, block]
        rms = lax.rsqrt(summed[:parts] / features + 1e-05)
        return [rms, rms * rms * rms * summed[parts:] / features]

    scales = turned(jnp.concatenate(row_scales(core) + row_scales(1 - core), axis=0))

    def scale_column(first_lane):
        return jnp.concatenate(
            [
                jnp.broadcast_to(scales[:, i : i + 1], (DH, DH))
                for i in range(first_lane, first_lane + parts)
            ],
            axis=0,
        )

    rms_col, coef_col = scale_column(0), scale_column(parts)
    rms_par, coef_par = scale_column(2 * parts), scale_column(3 * parts)

    def gradient(h):
        grad = (rms_col * gn[:, lanes(h)] - att[:, lanes(h)] * coef_col).astype(BF16)
        gb[:, lanes(h)] = grad
        return grad

    r_sems = fresh()
    for i in range(HALF):
        h = HALF * core + i
        r_own[core, part(i)] = nn(wqt[h], gradient(h)).reshape(per_head, rows, DH)
        grad = (rms_par * x_in[i, 2] - att_par[i] * coef_par).astype(BF16)
        r_par[part(i)] = nn(wqt_par[i], grad).reshape(per_head, rows, DH)
        stage_chip(r_own, r_par, r_chip, r_zin, i, r_sems, True)
    for i in range(HALF):
        h = HALF * (1 - core) + i
        arrived(f_copies[i])
        attend(h, state_b(f_ent, 1 - core, i))
        gradient(h)

    def back(h):
        grad = gb[:, lanes(h)]
        entering = state_b(f_ent, h // HALF, h % HALF)
        upper = []
        for t in range(0, BLOCK, TILE):
            seen = t + TILE
            here = slice(t, seen)
            weights = (nt(grad[here], v[:seen, lanes(h)]) * mask[h, here, :seen]).astype(BF16)
            upper.append(weights)
            dq[here, lanes(h)] = (
                nn(weights, k[:seen, lanes(h)]) + columns[1, h, here, :] * nt(grad[here], entering)
            ).astype(BF16)
        gt = grad.T
        for s in range(0, BLOCK, TILE):
            here = slice(s, s + TILE)
            key = value = None
            for t in range(s, BLOCK, TILE):
                there = slice(t, t + TILE)
                one_key = nn(qt[h, :, there], upper[t // TILE][:, here])
                one_value = nn(gt[:, there], fw[h, there, here])
                key = one_key if key is None else key + one_key
                value = one_value if value is None else value + one_value
            dki[here, lanes(h)] = key.T
            dvi[here, lanes(h)] = value.T

    for h in range(HEADS):
        dg[:, lanes(h)] = (gg[:, lanes(h)] * att[:, lanes(h)] * rms_col).astype(BF16)
    back(0)
    r_sems = stage_fold(r_zin, r_pre, r_back, r_sems, True)
    back(1)
    back(2)
    back(3)
    r_copies = [
        stage_split(r_own, r_par, r_back, r_ent, r_pair, i, r_sems, True)
        for i in range(HALF)
    ]
    for i in range(HALF):
        here = lanes(HALF * core + i)
        leaving = state_b(r_ent, core, i)
        dk[:, here] = (dki[:, here] + nt(wv[:, here], leaving)).astype(BF16)
        dv[:, here] = (dvi[:, here] + nn(wk[:, here], leaving)).astype(BF16)
    for i in range(HALF):
        arrived(r_copies[i])
    for mine, span in sent:
        pltpu.make_async_copy(span, span, send_sem.at[mine]).wait()


def finish(
    dq_in, dg_in, dk_in, dv_in, dki, dvi, wk, wv, ent,
    dq_hbm, dk_hbm, dv_hbm, dg_hbm, dk, dv, sem,
):
    core = lax.axis_index("ctx") % 2
    copies = []

    def store(src, dst):
        copy = pltpu.make_async_copy(src, dst, sem.at[len(copies)])
        copy.start(priority=len(copies) % 2)
        copies.append(copy)

    for first in range(0, BLOCK, TILE):
        here = pl.ds(first, TILE)
        store(dq_in.at[here], dq_hbm.at[here])
        store(dg_in.at[here], dg_hbm.at[here])
    mine = pl.ds(pl.multiple_of(core * HALF * DH, DH), HALF * DH)
    store(dk_in.at[:, mine], dk_hbm.at[:, mine])
    store(dv_in.at[:, mine], dv_hbm.at[:, mine])
    for i in range(HALF):
        h = HALF * (1 - core) + i
        leaving = ent[h].astype(BF16)
        dk[i] = (dki[:, lanes(h)] + nt(wv[:, lanes(h)], leaving)).astype(BF16)
        store(dk.at[i], dk_hbm.at[:, lanes(h)])
        dv[i] = (dvi[:, lanes(h)] + nn(wk[:, lanes(h)], leaving)).astype(BF16)
        store(dv.at[i], dv_hbm.at[:, lanes(h)])
    for copy in copies:
        copy.wait()


def build(nx, nz, nh):
    chips = nx * nz
    rows = HALF * DH // chips
    wide = (BLOCK, HEADS * DH)
    per_head = (HEADS, BLOCK, DH)

    def vmem(shape, dtype=F32):
        return pltpu.VMEM(shape, dtype)

    shards, halves = vmem((chips, rows, DH)), vmem((HALF, chips, rows, DH))
    scratch = (
        [vmem(wide, BF16)] * 5
        + [vmem((HEADS, BLOCK)), vmem((1, HEADS * DH))]
        + [vmem((3, 8, BLOCK)), vmem((BLOCK, DH)), vmem((3,) + per_head)]
        + [vmem((HEADS, DH, BLOCK), BF16)] * 2
        + [vmem(per_head, BF16)]
        + [vmem((HEADS, BLOCK, BLOCK)), vmem((HEADS, BLOCK, BLOCK), BF16)]
        + [vmem(wide)] * 3
        + [vmem(wide, BF16)]
        + [vmem((8, DH))] * 2
        + [vmem((chips, 8, DH))] * 2
        + [vmem((HALF, 3, BLOCK, DH))] * 2
        + [vmem((HALF, BLOCK, DH)), vmem((HALF, BLOCK, DH), BF16)]
        + [vmem((HALF, DH, BLOCK), BF16)]
        + [halves, shards, shards, shards, shards, halves, shards, shards]
        + [halves, shards, shards, shards, shards, shards, shards]
        + [vmem((2, 8, DH)), vmem((2 * nh, 2, 8, DH))]
        + [pltpu.SemaphoreType.DMA((7,))]
        + [pltpu.SemaphoreType.DMA((18,))] * 2
    )
    any_space = pl.BlockSpec(memory_space=pl.ANY)
    in_vmem = pl.BlockSpec(memory_space=pltpu.VMEM)

    def local(q, k, v, gate, gout, log_decay, gain):
        made = pl.pallas_call(
            functools.partial(kernel, nx, nz, nh),
            out_shape=[kept(wide, BF16)] * 4
            + [kept(wide, F32)] * 2
            + [kept(wide, BF16)] * 2
            + [kept((HALF, chips, rows, DH), F32)],
            in_specs=[any_space] * 7,
            out_specs=[in_vmem] * 9,
            scratch_shapes=scratch,
            compiler_params=pltpu.CompilerParams(
                collective_id=0, has_side_effects=True, vmem_limit_bytes=36 * 2**20
            ),
        )(*placed(
            (q, k, v, gate, gout, log_decay.T, gain.reshape(1, HEADS * DH)), pltpu.HBM
        ))
        made = list(made)
        made[-1] = made[-1].reshape(HEADS, DH, DH)
        return tuple(
            pl.pallas_call(
                finish,
                out_shape=[jax.ShapeDtypeStruct(wide, BF16)] * 4,
                in_specs=[in_vmem] * 9,
                out_specs=[any_space] * 4,
                scratch_shapes=[vmem((HALF, BLOCK, DH), BF16)] * 2
                + [pltpu.SemaphoreType.DMA((10,))],
                compiler_params=pltpu.CompilerParams(vmem_limit_bytes=8 * 2**20),
            )(*placed(made, pltpu.VMEM))
        )

    return local


def solution(mesh):
    nx, nz = NX, NZ
    if mesh.shape["ctx"] != 2 * nx * nz:
        nx = nz = 2
    part = P("ctx", "head")
    return jax.shard_map(
        build(nx, nz, mesh.shape["head"]),
        mesh=mesh,
        in_specs=(part,) * 6 + (P("head"),),
        out_specs=(part,) * 4,
        check_vma=False,
    )
```
